256 devices in a mesh: pool: 8 (over z_hi, core), tp: 32 (over x, z_lo, y).
Axes of the slice: x: 4, y: 4, z: 8 (z_hi: 4, z_lo: 2; z = z_hi * 2 + z_lo), core: 2. Of those that a mesh axis runs over, the one named last changes fastest.
Arguments:
- hidden: bfloat16 [2048, 8192], P(('pool', 'tp'))
- norm_gain: float32 [8192], replicated, may hold values from 0.1 to 1.9
- start_positions: int32 [32], P('pool'), may hold values from 256 to 4095
- draft_lengths: int32 [32], P('pool'), may hold values from 1 to 64
- query_weight: bfloat16 [8192, 8192], P(None, 'tp'), may hold values from -0.0625 to 0.0625
- w_keyvalue: bfloat16 [32, 8192, 256], P('tp'), as said below
- output_weight: bfloat16 [8192, 8192], P('tp'), may hold values from -0.0625 to 0.0625
- kv_cache: bfloat16 [32, 256, 32, 256], P('pool', None, 'tp'), as said below
- a_query: bfloat16 [8192, 64], P(('tp', 'pool')), may hold values from -0.0625 to 0.0625
- b_query: bfloat16 [64, 8192], P(None, ('tp', 'pool')), may hold values from -0.75 to 0.75
- a_key: bfloat16 [8192, 64], P(('tp', 'pool')), may hold values from -0.0625 to 0.0625
- b_key: bfloat16 [64, 1024], P(None, ('tp', 'pool')), may hold values from -0.75 to 0.75
- a_value: bfloat16 [8192, 64], P(('tp', 'pool')), may hold values from -0.0625 to 0.0625
- b_value: bfloat16 [64, 1024], P(None, ('tp', 'pool')), may hold values from -0.75 to 0.75
- a_out: bfloat16 [8192, 64], P(('tp', 'pool')), may hold values from -0.0625 to 0.0625
- b_out: bfloat16 [64, 8192], P(None, ('tp', 'pool')), may hold values from -0.75 to 0.75
Outputs:
- updated: bfloat16 [2048, 8192], P(('pool', 'tp'))
The draws below stay inside these ranges and needn't reach their ends.
Inputs may be any that keep to these rules, and one draw needn't show every extreme that they name: `w_keyvalue`: blocks t and u along the first dimension are equal when t // 4 == u // 4; block t holds the key columns (first 128) and value columns of key-value head t // 4. `kv_cache`: entries t and u along the third dimension are equal when t // 4 == u // 4; the first 128 entries are the key, the rest the value of key-value head t // 4.
All inputs are finite; a program needn't handle non-finite values.
Results may differ from the reference program's by a relative error of at most 0.02.
Values may be sent and summed in bfloat16 or wider, within the bound.
No kernel may reach another device: no remote copies, remote signals or barrier semaphores. Data moves between devices by JAX's collectives and lax.ppermute only.
A program may use at most 128 MiB of HBM per device.

```python
import math
import jax
import jax.numpy as jnp
from jax import lax

D = 8192
HEADS = 64
KV_HEADS = 8
HEAD_DIM = 128
RANK = 64
VERIFY = 64
SEQS = 4
CTX = 256
ALL_SEQS = 32
N_POOL = 8
N_TP = 32


def draw_hidden(key, part):
    key = jax.random.fold_in(key, 11)
    first_key, second_key, third_key = jax.random.split(key, 3)
    total_rows = N_POOL * SEQS * VERIFY
    col_scale = jnp.exp(jax.random.uniform(third_key, (1, D), jnp.float32, math.log(0.5), math.log(2.0)))
    row_scale = jnp.exp(jax.random.uniform(second_key, (total_rows, 1), jnp.float32, math.log(0.3), math.log(3.0)))
    frozen_base = jax.random.normal(first_key, (total_rows, D), jnp.float32)
    return (frozen_base * row_scale * col_scale).astype(jnp.bfloat16)


def draw_draft_lengths(key, part):
    key = jax.random.fold_in(key, 23)
    first_key, second_key = jax.random.split(key, 2)
    seq_total = N_POOL * SEQS
    lengths = jax.random.randint(first_key, (seq_total,), 1, VERIFY + 1)
    chosen = jax.random.randint(second_key, (), 0, seq_total)
    lengths = lengths.at[chosen].set(VERIFY)
    return lengths.astype(jnp.int32)


def draw_w_keyvalue(key, part):
    key = jax.random.fold_in(key, 37)
    frozen_base = jax.random.normal(key, (KV_HEADS, D, 2 * HEAD_DIM), jnp.float32) * D ** (-0.5)
    return jnp.repeat(frozen_base, N_TP // KV_HEADS, axis=0).astype(jnp.bfloat16)


def draw_kv_cache(key, part):
    key = jax.random.fold_in(key, 53)
    first_key = jax.random.fold_in(key, 0)
    seq_total = N_POOL * SEQS
    shape = (seq_total, CTX, KV_HEADS, 2 * HEAD_DIM)
    frozen_base = jax.random.normal(first_key, shape, jnp.float32)
    return jnp.repeat(frozen_base, N_TP // KV_HEADS, axis=2).astype(jnp.bfloat16)


def with_ends(entries, own_key, least, largest):
    shape = entries.shape
    index_at = [jax.random.randint(jax.random.fold_in(own_key, axis), (), 0, shape[axis]) for axis in range(len(shape))]
    entries = entries.at[tuple(index_at)].set(least)
    longest = shape.index(max(shape))
    index_at[longest] = (index_at[longest] + 1) % shape[longest]
    return entries.at[tuple(index_at)].set(largest)


def block_levels(key, extent, shards, least, top_value):
    def one(position, blocks):
        heights = jax.random.uniform(jax.random.fold_in(jax.random.fold_in(key, 6), position), (blocks,), jnp.float32, least / len(shards), top_value / len(shards))
        return jnp.repeat(jnp.exp(heights), extent[position] // blocks).reshape((-1,) + (1,) * (len(extent) - position - 1))

    gain = one(*shards[0])
    for cut in shards[1:]:
        gain = gain * one(*cut)
    return gain


def bell_draw(key, dims, deviation, most, cuts=(), held_as=jnp.bfloat16):
    array = jax.random.normal(key, dims, jnp.float32) * deviation
    if len(cuts) > 0:
        array = block_levels(key, dims, cuts, -0.22, 0.18) * array
    return jnp.clip(array, min=-most, max=most).astype(held_as)


def setup_inputs(seed: int = 0) -> dict:
    arg_keys = jax.random.split(jax.random.key(seed), 17)
    return {
        "hidden": draw_hidden(jax.random.fold_in(arg_keys[16], 71), 0),
        "norm_gain": jnp.clip(1.0 + 0.18 * jax.random.normal(arg_keys[1], (D,), jnp.float32), 0.1, 1.9),
        "start_positions": with_ends(jax.random.randint(arg_keys[2], (ALL_SEQS,), CTX, 4096), jax.random.fold_in(arg_keys[2], 1), CTX, 4095).astype(jnp.int32),
        "draft_lengths": draw_draft_lengths(jax.random.fold_in(arg_keys[16], 71), 0),
        "query_weight": bell_draw(arg_keys[4], (D, HEADS * HEAD_DIM), D ** -0.5, 0.0625, ((1, 32),)),
        "w_keyvalue": draw_w_keyvalue(jax.random.fold_in(arg_keys[16], 71), 0),
        "output_weight": bell_draw(arg_keys[6], (HEADS * HEAD_DIM, D), (HEADS * HEAD_DIM) ** -0.5, 0.0625, ((0, 32),)),
        "kv_cache": draw_kv_cache(jax.random.fold_in(arg_keys[16], 71), 0),
        "a_query": bell_draw(arg_keys[8], (D, RANK), D ** -0.5, 0.0625, ((0, 256),)),
        "b_query": bell_draw(arg_keys[9], (RANK, HEADS * HEAD_DIM), RANK ** -0.5, 0.75, ((1, 256),)),
        "a_key": bell_draw(arg_keys[10], (D, RANK), D ** -0.5, 0.0625, ((0, 256),)),
        "b_key": bell_draw(arg_keys[11], (RANK, KV_HEADS * HEAD_DIM), RANK ** -0.5, 0.75, ((1, 256),)),
        "a_value": bell_draw(arg_keys[12], (D, RANK), D ** -0.5, 0.0625, ((0, 256),)),
        "b_value": bell_draw(arg_keys[13], (RANK, KV_HEADS * HEAD_DIM), RANK ** -0.5, 0.75, ((1, 256),)),
        "a_out": bell_draw(arg_keys[14], (HEADS * HEAD_DIM, RANK), (HEADS * HEAD_DIM) ** -0.5, 0.0625, ((0, 256),)),
        "b_out": bell_draw(arg_keys[15], (RANK, D), RANK ** -0.5, 0.75, ((1, 256),)),
    }


adapter_scale = 1.0
rope_base = 1000000.0
norm_eps = 1e-06

def rotate(values, places):
    half_dim = values.shape[-1] // 2
    freqs = jnp.exp(jnp.arange(half_dim, dtype=jnp.float32) * (-2.0 * math.log(rope_base) / values.shape[-1]))
    angles = places.astype(jnp.float32)[:, None] * freqs[None, :]
    cosine = jnp.cos(angles)[:, None, :]
    sine = jnp.sin(angles)[:, None, :]
    first = values[..., :half_dim]
    second = values[..., half_dim:]
    return jnp.concatenate([first * cosine - second * sine, second * cosine + first * sine], axis=-1)

def adapted(inputs, frozen, down, upward_factor):
    frozen_base = jnp.dot(inputs, frozen, preferred_element_type=jnp.float32)
    inner_product = jnp.dot(inputs, down, preferred_element_type=jnp.float32)
    return frozen_base + adapter_scale * jnp.dot(inner_product, upward_factor.astype(jnp.float32), precision=lax.Precision.HIGHEST)

def attend(inputs):
    query, keys, values, cached, length = inputs
    scale = 1.0 / math.sqrt(HEAD_DIM)
    grouped = query.reshape(VERIFY, KV_HEADS, HEADS // KV_HEADS, HEAD_DIM).astype(jnp.float32)
    cache_scores = jnp.einsum('qkgd,ckd->kgqc', grouped, cached[..., :HEAD_DIM].astype(jnp.float32)) * scale
    draft_scores = jnp.einsum('qkgd,jkd->kgqj', grouped, keys.astype(jnp.float32)) * scale
    places = jnp.arange(VERIFY, dtype=jnp.int32)
    allowed = (places[None, :] <= places[:, None]) & (places[None, :] < length)
    draft_scores = jnp.where(allowed, draft_scores, -1e+30)
    scores = jnp.concatenate([cache_scores, draft_scores], axis=-1)
    highest = lax.optimization_barrier(jnp.max(scores, axis=-1, keepdims=True))
    powers = jnp.exp(scores - highest)
    weights = (powers / lax.optimization_barrier(jnp.sum(powers, axis=-1, keepdims=True))).astype(jnp.bfloat16)
    mixed = jnp.einsum('kgqc,ckd->qkgd', weights[..., :CTX].astype(jnp.float32), cached[..., HEAD_DIM:].astype(jnp.float32))
    mixed = mixed + jnp.einsum('kgqj,jkd->qkgd', weights[..., CTX:].astype(jnp.float32), values.astype(jnp.float32))
    active = (places < length).astype(jnp.float32)
    mixed = mixed * active[:, None, None, None]
    return mixed.reshape(VERIFY, HEADS * HEAD_DIM).astype(jnp.bfloat16)

def reference(hidden, norm_gain, start_positions, draft_lengths, query_weight, w_keyvalue, output_weight, kv_cache, a_query, b_query, a_key, b_key, a_value, b_value, a_out, b_out):
    row_float = hidden.astype(jnp.float32)
    normed = (row_float * lax.rsqrt(lax.optimization_barrier(jnp.mean(row_float * row_float, axis=-1, keepdims=True)) + norm_eps) * norm_gain).astype(jnp.bfloat16)
    head_group = N_TP // KV_HEADS
    head_blocks = w_keyvalue[::head_group]
    w_key = jnp.transpose(head_blocks[:, :, :HEAD_DIM], (1, 0, 2)).reshape(D, KV_HEADS * HEAD_DIM)
    w_value = jnp.transpose(head_blocks[:, :, HEAD_DIM:], (1, 0, 2)).reshape(D, KV_HEADS * HEAD_DIM)
    query = adapted(normed, query_weight, a_query, b_query)
    keys = adapted(normed, w_key, a_key, b_key)
    values = adapted(normed, w_value, a_value, b_value)
    total_rows = hidden.shape[0]
    seq_total = start_positions.shape[0]
    places = (start_positions[:, None] + jnp.arange(VERIFY, dtype=jnp.int32)[None, :]).reshape(total_rows)
    query = rotate(query.reshape(total_rows, HEADS, HEAD_DIM), places).astype(jnp.bfloat16)
    keys = rotate(keys.reshape(total_rows, KV_HEADS, HEAD_DIM), places).astype(jnp.bfloat16)
    values = values.reshape(total_rows, KV_HEADS, HEAD_DIM).astype(jnp.bfloat16)
    cached = kv_cache[:, :, ::head_group, :]
    attended = lax.map(attend, (query.reshape(seq_total, VERIFY, HEADS, HEAD_DIM), keys.reshape(seq_total, VERIFY, KV_HEADS, HEAD_DIM), values.reshape(seq_total, VERIFY, KV_HEADS, HEAD_DIM), cached, draft_lengths))
    attended = attended.reshape(total_rows, HEADS * HEAD_DIM)
    branch = adapted(attended, output_weight, a_out, b_out)
    return (row_float + branch).astype(jnp.bfloat16)
```

```python
import math

import jax
import jax.numpy as jnp
from jax import lax
from jax.sharding import Mesh, PartitionSpec as P

VERIFY = 64
HEAD_DIM = 128

adapter_scale = 1.0
rope_base = 1000000.0
norm_eps = 1e-06

AXES = ("zh", "core", "x", "zl", "y")
TP = ("x", "zl", "y")
POOL = ("zh", "core")


def rotate(values, places):
    half_dim = values.shape[-1] // 2
    freqs = jnp.exp(
        jnp.arange(half_dim, dtype=jnp.float32) * (-2.0 * math.log(rope_base) / values.shape[-1])
    )
    angles = places.astype(jnp.float32)[:, None] * freqs[None, :]
    cosine = jnp.cos(angles)[:, None, :]
    sine = jnp.sin(angles)[:, None, :]
    first = values[..., :half_dim]
    second = values[..., half_dim:]
    return jnp.concatenate(
        [first * cosine - second * sine, second * cosine + first * sine], axis=-1
    )


def dot32(left, right):
    return jnp.dot(left, right, preferred_element_type=jnp.float32)


def spread(block, axes):
    count = lax.axis_size(axes)
    return lax.all_to_all(jnp.broadcast_to(block[None], (count,) + block.shape), axes, 0, 0)


def shards(
    hidden,
    norm_gain,
    start_positions,
    draft_lengths,
    query_weight,
    w_keyvalue,
    output_weight,
    kv_cache,
    a_query,
    b_query,
    a_key,
    b_key,
    a_value,
    b_value,
    a_out,
    b_out,
):
    shard_index = lax.axis_index(TP)
    head_dim = w_keyvalue.shape[2] // 2
    query_width = query_weight.shape[1]
    heads_here = query_width // head_dim
    seq_count = start_positions.shape[0]
    cache_len = kv_cache.shape[1]
    row_float = hidden.astype(jnp.float32)
    normed = (
        row_float
        * lax.rsqrt(jnp.mean(row_float * row_float, axis=-1, keepdims=True) + norm_eps)
        * norm_gain
    ).astype(jnp.bfloat16)

    packed = jnp.concatenate(
        [
            jnp.concatenate([a_query, a_key], axis=1),
            jnp.concatenate([a_value, a_out], axis=1),
            jnp.concatenate([b_query.T, b_out.T], axis=1),
            jnp.concatenate([b_key.T, b_value.T], axis=1),
        ],
        axis=0,
    )
    pooled = spread(packed, POOL)
    down_first = pooled[:, 0:32].reshape(256, 128)
    down_second = pooled[:, 32:64].reshape(256, 128)
    up_wide = pooled[:, 64:96].reshape(256, 128)
    up_narrow = pooled[:, 96:100].reshape(32, 128)
    down_in = jnp.concatenate([down_first, down_second[:, :64]], axis=1)
    down_out = down_second[:, 64:]
    query_up = up_wide[:, :64]
    narrow = spread(up_narrow, "y").reshape(128, 128)
    key_up = narrow[:, :64]
    value_up = narrow[:, 64:]
    out_up = spread(up_wide[:, 64:], TP).reshape(8192, 64)

    rows = spread(normed, TP).reshape(256, 8192)
    mine = lax.dynamic_slice_in_dim(rows, shard_index * 256, 256, 1)
    inner = dot32(mine, down_in).astype(jnp.bfloat16).reshape(32, 8, 192)
    inner = lax.all_to_all(inner, TP, 0, 0).astype(jnp.float32).sum(0).astype(jnp.bfloat16)
    inner = spread(inner, TP).reshape(256, 192)

    def up(inner, factor):
        return lax.dot_general(
            inner, factor, (((1,), (1,)), ((), ())), preferred_element_type=jnp.float32
        )

    query = dot32(rows, query_weight) + adapter_scale * up(inner[:, :64], query_up)
    pair = dot32(rows, w_keyvalue[0])
    keys = pair[:, :head_dim] + adapter_scale * up(inner[:, 64:128], key_up)
    values = pair[:, head_dim:] + adapter_scale * up(inner[:, 128:], value_up)
    group_rows = 256
    draft_places = jnp.arange(VERIFY, dtype=jnp.int32)
    places = (start_positions[:, None] + draft_places[None, :]).reshape(group_rows)
    query = rotate(query.reshape(group_rows, heads_here, head_dim), places).astype(jnp.bfloat16)
    keys = rotate(keys.reshape(group_rows, 1, head_dim), places).astype(jnp.bfloat16)
    values = values.astype(jnp.bfloat16)
    query_seq = query.reshape(seq_count, VERIFY, heads_here, head_dim)
    key_seq = keys.reshape(seq_count, VERIFY, head_dim)
    value_seq = values.reshape(seq_count, VERIFY, head_dim)
    cached = kv_cache[:, :, 0, :]
    scale = 1.0 / math.sqrt(head_dim)
    cache_scores = (
        jnp.einsum(
            "sqhd,scd->shqc", query_seq, cached[..., :head_dim], preferred_element_type=jnp.float32
        )
        * scale
    )
    draft_scores = (
        jnp.einsum("sqhd,sjd->shqj", query_seq, key_seq, preferred_element_type=jnp.float32) * scale
    )
    allowed = (draft_places[None, None, :] <= draft_places[None, :, None]) & (
        draft_places[None, None, :] < draft_lengths[:, None, None]
    )
    draft_scores = jnp.where(allowed[:, None, :, :], draft_scores, -1e30)
    scores = jnp.concatenate([cache_scores, draft_scores], axis=-1)
    highest = jnp.max(scores, axis=-1, keepdims=True)
    powers = jnp.exp(scores - highest)
    weights = (powers / jnp.sum(powers, axis=-1, keepdims=True)).astype(jnp.bfloat16)
    mixed = jnp.einsum(
        "shqc,scd->sqhd",
        weights[..., :cache_len],
        cached[..., head_dim:],
        preferred_element_type=jnp.float32,
    )
    mixed = mixed + jnp.einsum(
        "shqj,sjd->sqhd", weights[..., cache_len:], value_seq, preferred_element_type=jnp.float32
    )
    active = (draft_places[None, :] < draft_lengths[:, None]).astype(jnp.float32)
    mixed = mixed * active[:, :, None, None]
    attended = mixed.reshape(group_rows, query_width).astype(jnp.bfloat16)

    out_inner = dot32(attended, down_out).astype(jnp.bfloat16)
    partial = (dot32(attended, output_weight) + adapter_scale * up(out_inner, out_up)).astype(
        jnp.bfloat16
    )
    partial = lax.all_to_all(partial.reshape(32, 8, 8192), TP, 0, 0)
    branch = partial.astype(jnp.float32).sum(0)
    return (row_float + branch).astype(jnp.bfloat16)


def solution(mesh):
    fine = Mesh(mesh.devices.reshape(4, 2, 4, 2, 4), AXES)
    both = ("x", "zl", "y", "zh", "core")
    in_specs = (
        P(AXES, None),
        P(),
        P(POOL),
        P(POOL),
        P(None, TP),
        P(TP, None, None),
        P(TP, None),
        P(POOL, None, TP, None),
        P(both, None),
        P(None, both),
        P(both, None),
        P(None, both),
        P(both, None),
        P(None, both),
        P(both, None),
        P(None, both),
    )
    out_specs = P(AXES, None)
    return jax.shard_map(shards, mesh=fine, in_specs=in_specs, out_specs=out_specs, check_vma=False)
```

```python
import math

import jax
import jax.numpy as jnp
from jax import lax
from jax.sharding import Mesh, PartitionSpec as P

VERIFY = 64
HEAD_DIM = 128

adapter_scale = 1.0
rope_base = 1000000.0
norm_eps = 1e-06

AXES = ("zh", "core", "x", "zl", "y")
TP = ("x", "zl", "y")
POOL = ("zh", "core")


def rotate(values, places):
    half_dim = values.shape[-1] // 2
    freqs = jnp.exp(
        jnp.arange(half_dim, dtype=jnp.float32) * (-2.0 * math.log(rope_base) / values.shape[-1])
    )
    angles = places.astype(jnp.float32)[:, None] * freqs[None, :]
    cosine = jnp.cos(angles)[:, None, :]
    sine = jnp.sin(angles)[:, None, :]
    first = values[..., :half_dim]
    second = values[..., half_dim:]
    return jnp.concatenate(
        [first * cosine - second * sine, second * cosine + first * sine], axis=-1
    )


def dot32(left, right):
    return jnp.dot(left, right, preferred_element_type=jnp.float32)


def permute(block, source_to_target):
    return lax.ppermute(block, AXES, source_to_target)


def pairs(move):
    spots = [
        (zh, core, x, zl, y)
        for zh in range(4)
        for core in range(2)
        for x in range(4)
        for zl in range(2)
        for y in range(4)
    ]
    place = {spot: number for number, spot in enumerate(spots)}
    return [(place[spot], place[move(*spot)]) for spot in spots]


def last_shift(s):
    return pairs(
        lambda h, c, x, z, y: (h, c, (x + s) % 4, z, y) if c == 0 else (h, c, x, z, (y + s) % 4)
    )


def middle_shift(s):
    return pairs(
        lambda h, c, x, z, y: (h, c, x, z, (y + s) % 4) if c == 0 else (h, c, (x + s) % 4, z, y)
    )


def pool_shift(s):
    return pairs(lambda h, c, x, z, y: ((h + s) % 4, c, x, z, y))


def z_swap():
    return pairs(lambda h, c, x, z, y: (h, c, x, 1 - z, y))


def core_swap():
    return pairs(lambda h, c, x, z, y: (h, 1 - c, x, z, y))


def placed(blocks, here):
    count = len(blocks)
    out = jnp.zeros((count,) + blocks[0].shape, blocks[0].dtype)
    for s, block in enumerate(blocks):
        out = lax.dynamic_update_index_in_dim(out, block, (here - s) % count, 0)
    return out


def gather4(block, shift, here):
    return placed([block] + [permute(block, shift(s)) for s in (1, 2, 3)], here)


def pick(blocks, index):
    return lax.dynamic_index_in_dim(blocks, index, 0, keepdims=False)


def up(inner, factor):
    return lax.dot_general(
        inner, factor, (((1,), (1,)), ((), ())), preferred_element_type=jnp.float32
    )


def group_sum(part):
    both = (part + permute(part.astype(jnp.bfloat16), z_swap())).astype(jnp.bfloat16)
    return sum(
        other.astype(jnp.float32)
        for other in [both] + [permute(both, middle_shift(s)) for s in (1, 2, 3)]
    )


def shards(
    hidden,
    norm_gain,
    start_positions,
    draft_lengths,
    query_weight,
    w_keyvalue,
    output_weight,
    kv_cache,
    a_query,
    b_query,
    a_key,
    b_key,
    a_value,
    b_value,
    a_out,
    b_out,
):
    zh, core, x, zl, y = (lax.axis_index(name) for name in AXES)
    first_core = core == 0
    last = jnp.where(first_core, x, y)
    middle = jnp.where(first_core, y, x)
    head_dim = w_keyvalue.shape[2] // 2
    query_width = query_weight.shape[1]
    heads_here = query_width // head_dim
    seq_count = start_positions.shape[0]
    cache_len = kv_cache.shape[1]
    half = jnp.bfloat16

    def tp_index(k):
        return jnp.where(first_core, k * 8 + zl * 4 + y, x * 8 + zl * 4 + k)

    row_float = hidden.astype(jnp.float32)
    normed = (
        row_float
        * lax.rsqrt(jnp.mean(row_float * row_float, axis=-1, keepdims=True) + norm_eps)
        * norm_gain
    ).astype(half)

    pair = placed([normed, permute(normed, z_swap())], zl).reshape(16, 8192)
    eight = gather4(pair, middle_shift, middle).reshape(64, 8192)
    arrived = [eight] + [permute(eight, last_shift(s)) for s in (1, 2, 3)]

    packed = jnp.concatenate(
        [
            jnp.concatenate([a_query, a_key], axis=1),
            jnp.concatenate([a_value, a_out], axis=1),
            jnp.concatenate([b_query.T, b_out.T], axis=1),
            jnp.concatenate([b_key.T, b_value.T], axis=1),
            jnp.zeros((4, 128), half),
        ],
        axis=0,
    )
    pooled = gather4(packed, pool_shift, zh)
    pooled = jnp.swapaxes(placed([pooled, permute(pooled, core_swap())], core), 0, 1)
    pooled = pooled.reshape(8, 104, 128)
    wide = gather4(pooled, last_shift, last)
    down_first = wide[:, :, 0:32].reshape(1024, 128)
    down_second = wide[:, :, 32:64].reshape(1024, 128)
    out_up = wide[:, :, 64:96, 64:].reshape(4, 256, 64)
    down_out = pooled[:, 32:64, 64:].reshape(256, 64)
    query_up = pooled[:, 64:96, :64].reshape(256, 64)
    narrow = wide[:, :, 96:100].reshape(128, 128)
    narrow = jnp.where(first_core, permute(narrow, core_swap()), narrow)
    key_up = narrow[:, :64]
    value_up = narrow[:, 64:]

    mine = jnp.concatenate(
        [lax.dynamic_slice_in_dim(eight, tp_index(k) * 256, 256, 1) for k in range(4)], axis=1
    )
    inner = jnp.concatenate([dot32(mine, down_first), dot32(mine, down_second)[:, :64]], axis=1)
    inner = group_sum(inner).astype(half)
    inners = [inner] + [permute(inner, last_shift(s)) for s in (1, 2, 3)]

    def project(block, inner):
        query = dot32(block, query_weight) + adapter_scale * up(inner[:, :64], query_up)
        both = dot32(block, w_keyvalue[0])
        keys = both[:, :head_dim] + adapter_scale * up(inner[:, 64:128], key_up)
        values = both[:, head_dim:] + adapter_scale * up(inner[:, 128:], value_up)
        return jnp.concatenate([query, keys, values], axis=1)

    projected = placed(
        [project(block, inner) for block, inner in zip(arrived, inners)], last
    ).reshape(4, 4, 16, query_width + 2 * head_dim)
    projected = jnp.where(first_core, projected, jnp.swapaxes(projected, 0, 1))
    projected = projected.reshape(seq_count * VERIFY, query_width + 2 * head_dim)
    query = projected[:, :query_width]
    keys = projected[:, query_width : query_width + head_dim]
    values = projected[:, query_width + head_dim :]
    draft_places = (
        jnp.arange(VERIFY, dtype=jnp.int32).reshape(2, 4, 8).transpose(1, 0, 2).reshape(VERIFY)
    )
    group_rows = seq_count * VERIFY
    places = (start_positions[:, None] + draft_places[None, :]).reshape(group_rows)
    query = rotate(query.reshape(group_rows, heads_here, head_dim), places).astype(half)
    keys = rotate(keys.reshape(group_rows, 1, head_dim), places).astype(half)
    values = values.astype(half)
    query_seq = query.reshape(seq_count, VERIFY, heads_here, head_dim)
    key_seq = keys.reshape(seq_count, VERIFY, head_dim)
    value_seq = values.reshape(seq_count, VERIFY, head_dim)
    cached = kv_cache[:, :, 0, :]
    scale = 1.0 / math.sqrt(head_dim)
    cache_scores = (
        jnp.einsum(
            "sqhd,scd->shqc", query_seq, cached[..., :head_dim], preferred_element_type=jnp.float32
        )
        * scale
    )
    draft_scores = (
        jnp.einsum("sqhd,sjd->shqj", query_seq, key_seq, preferred_element_type=jnp.float32) * scale
    )
    allowed = (draft_places[None, None, :] <= draft_places[None, :, None]) & (
        draft_places[None, None, :] < draft_lengths[:, None, None]
    )
    draft_scores = jnp.where(allowed[:, None, :, :], draft_scores, -1e30)
    scores = jnp.concatenate([cache_scores, draft_scores], axis=-1)
    highest = jnp.max(scores, axis=-1, keepdims=True)
    powers = jnp.exp(scores - highest)
    weights = (powers / jnp.sum(powers, axis=-1, keepdims=True)).astype(half)
    mixed = jnp.einsum(
        "shqc,scd->sqhd",
        weights[..., :cache_len],
        cached[..., head_dim:],
        preferred_element_type=jnp.float32,
    )
    mixed = mixed + jnp.einsum(
        "shqj,sjd->sqhd", weights[..., cache_len:], value_seq, preferred_element_type=jnp.float32
    )
    active = (draft_places[None, :] < draft_lengths[:, None]).astype(jnp.float32)
    mixed = mixed * active[:, :, None, None]
    attended = mixed.reshape(4, 4, 16, query_width).astype(half)
    attended = jnp.where(first_core, attended, jnp.swapaxes(attended, 0, 1))
    attended = attended.reshape(4, 64, query_width)

    out_inner = dot32(attended.reshape(256, query_width), down_out).astype(half).reshape(4, 64, 64)
    out_inner = sum(
        [pick(out_inner, last).astype(jnp.float32)]
        + [
            permute(pick(out_inner, (last + s) % 4), last_shift(s)).astype(jnp.float32)
            for s in (1, 2, 3)
        ]
    )
    out_inner = group_sum(out_inner).astype(half)

    sent = [
        permute(
            dot32(pick(attended, (last + s) % 4), output_weight).astype(half), last_shift(s)
        ).astype(jnp.float32)
        for s in (1, 2, 3)
    ]
    total = dot32(pick(attended, last), output_weight) + sum(sent)
    for k in range(4):
        at = tp_index(k) * 256
        total = lax.dynamic_update_slice_in_dim(
            total,
            lax.dynamic_slice_in_dim(total, at, 256, 1) + adapter_scale * up(out_inner, out_up[k]),
            at,
            1,
        )
    total = total.reshape(4, 16, 8192)
    total = pick(total, middle) + sum(
        permute(pick(total, (middle + s) % 4).astype(half), middle_shift(s)).astype(jnp.float32)
        for s in (1, 2, 3)
    )
    total = total.reshape(2, 8, 8192)
    branch = pick(total, zl) + permute(pick(total, 1 - zl).astype(half), z_swap()).astype(
        jnp.float32
    )
    return (row_float + branch).astype(half)


def solution(mesh):
    fine = Mesh(mesh.devices.reshape(4, 2, 4, 2, 4), AXES)
    both = ("x", "zl", "y", "zh", "core")
    in_specs = (
        P(AXES, None),
        P(),
        P(POOL),
        P(POOL),
        P(None, TP),
        P(TP, None, None),
        P(TP, None),
        P(POOL, None, TP, None),
        P(both, None),
        P(None, both),
        P(both, None),
        P(None, both),
        P(both, None),
        P(None, both),
        P(both, None),
        P(None, both),
    )
    out_specs = P(AXES, None)
    return jax.shard_map(shards, mesh=fine, in_specs=in_specs, out_specs=out_specs, check_vma=False)
```

```python
import math

import jax
import jax.numpy as jnp
from jax import lax
from jax.experimental import pallas as pl
from jax.experimental.pallas import tpu as pltpu
from jax.sharding import Mesh, PartitionSpec as P

VERIFY = 64
HEAD_DIM = 128

adapter_scale = 1.0
rope_base = 1000000.0
norm_eps = 1e-06

AXES = ("zh", "core", "x", "zl", "y")
TP = ("x", "zl", "y")
POOL = ("zh", "core")
SPOTS = [
    (zh, core, x, zl, y)
    for zh in range(4)
    for core in range(2)
    for x in range(4)
    for zl in range(2)
    for y in range(4)
]


def turns(places, width):
    half_dim = width // 2
    freqs = jnp.exp(
        jnp.arange(half_dim, dtype=jnp.float32) * (-2.0 * math.log(rope_base) / width)
    )
    angles = places.astype(jnp.float32)[:, None] * freqs[None, :]
    cosine, sine = jnp.cos(angles), jnp.sin(angles)
    return jnp.concatenate([cosine, cosine], axis=1), jnp.concatenate([-sine, sine], axis=1)


def dot32(left, right):
    return jnp.dot(left, right, preferred_element_type=jnp.float32)


def permute(block, source_to_target):
    return lax.ppermute(block, AXES, source_to_target)


def pairs(move):
    place = {spot: number for number, spot in enumerate(SPOTS)}
    return [(place[spot], place[move(*spot)]) for spot in SPOTS]


def last_shift(s):
    return pairs(
        lambda h, c, x, z, y: (h, c, (x + s) % 4, z, y) if c == 0 else (h, c, x, z, (y + s) % 4)
    )


def middle_shift(s):
    return pairs(
        lambda h, c, x, z, y: (h, c, x, z, (y + s) % 4) if c == 0 else (h, c, (x + s) % 4, z, y)
    )


def z_swap():
    return pairs(lambda h, c, x, z, y: (h, c, x, 1 - z, y))


def core_swap():
    return pairs(lambda h, c, x, z, y: (h, 1 - c, x, z, y))


def placed(blocks, here):
    count = len(blocks)
    out = jnp.zeros((count,) + blocks[0].shape, blocks[0].dtype)
    for s, block in enumerate(blocks):
        out = lax.dynamic_update_index_in_dim(out, block, (here - s) % count, 0)
    return out


def pick(blocks, index):
    return lax.dynamic_index_in_dim(blocks, index, 0, keepdims=False)


def spread(block, count, groups):
    return lax.all_to_all(
        jnp.broadcast_to(block[None], (count,) + block.shape),
        AXES,
        0,
        0,
        axis_index_groups=groups,
    )


def groups_of(key, order):
    found = {}
    for number, spot in enumerate(SPOTS):
        found.setdefault(key(*spot), []).append((order(*spot), number))
    return [[number for _, number in sorted(group)] for group in found.values()]


def pool_groups():
    return groups_of(lambda h, c, x, z, y: (x, z, y), lambda h, c, x, z, y: (h, c))


def last_groups():
    return groups_of(
        lambda h, c, x, z, y: (h, c, z, y) if c == 0 else (h, c, x, z),
        lambda h, c, x, z, y: x if c == 0 else y,
    )


def row_groups():
    return groups_of(
        lambda h, c, x, z, y: (h, c),
        lambda h, c, x, z, y: (x, z, y) if c == 0 else (y, z, x),
    )


def spec_smem():
    return pl.BlockSpec(memory_space=pltpu.SMEM)


def project_kernel(
    eight_ref, one_ref, left_ref, right_ref, three_ref, query_ref, pair_ref, out_ref, total
):
    step = pl.program_id(0)
    steps = pl.num_programs(0)

    @pl.when(step == 0)
    def _():
        total[...] = jnp.zeros_like(total)

    def add(two_ref):
        rows = jnp.concatenate(
            [eight_ref[...], one_ref[...], two_ref[...], three_ref[...]], axis=0
        )
        width = query_ref.shape[1]
        total[:, :width] += jnp.dot(rows, query_ref[...], preferred_element_type=jnp.float32)
        total[:, width:] += jnp.dot(rows, pair_ref[...], preferred_element_type=jnp.float32)

    @pl.when(step < steps // 2)
    def _():
        add(left_ref)

    @pl.when(step >= steps // 2)
    def _():
        add(right_ref)

    @pl.when(step == steps - 1)
    def _():
        out_ref[...] = total[...]


def project_rows(eight, one, left_2, right_2, three, query_weight, pair_weight):
    tile = 1024
    steps = eight.shape[1] // tile
    width = query_weight.shape[1]
    whole = pl.BlockSpec((64, tile), lambda j: (0, j))
    return pl.pallas_call(
        project_kernel,
        grid=(steps,),
        in_specs=[
            whole,
            whole,
            pl.BlockSpec((64, tile), lambda j: (0, jnp.minimum(j, steps // 2 - 1))),
            pl.BlockSpec((64, tile), lambda j: (0, jnp.maximum(j - steps // 2, 0))),
            whole,
            pl.BlockSpec((tile, width), lambda j: (j, 0)),
            pl.BlockSpec((tile, width), lambda j: (j, 0)),
        ],
        out_specs=pl.BlockSpec((256, 2 * width), lambda j: (0, 0)),
        out_shape=jax.ShapeDtypeStruct((256, 2 * width), jnp.float32),
        scratch_shapes=[pltpu.VMEM((256, 2 * width), jnp.float32)],
        compiler_params=pltpu.CompilerParams(vmem_limit_bytes=24 * 2**20),
        cost_estimate=pl.CostEstimate(
            flops=2 * 256 * 512 * 8192, bytes_accessed=12 * 2**20, transcendentals=0
        ),
    )(eight, one, left_2, right_2, three, query_weight, pair_weight)


def outer(left, right):
    return lax.dot_general(
        left, right, (((1,), (1,)), ((), ())), preferred_element_type=jnp.float32
    )


def attend_kernel(
    spot_ref,
    lengths_ref,
    frozen_ref,
    parts_ref,
    query_up_ref,
    key_up_ref,
    value_up_ref,
    cosine_ref,
    sine_ref,
    cache_ref,
    down_ref,
    ahead_ref,
    inner_ref,
    rows,
    found,
):
    half = jnp.bfloat16
    first_core = spot_ref[0] == 0
    last = spot_ref[1]
    for s in range(4):
        k = lax.rem(last - s + 4, 4)
        inner = parts_ref[k, 0].astype(jnp.float32)
        for part in range(1, 8):
            inner = inner + parts_ref[k, part].astype(jnp.float32)
        inner = inner.astype(half)
        frozen = frozen_ref[64 * s : 64 * s + 64]
        rows[k, :, :256] = frozen[:, :256] + adapter_scale * outer(inner[:, :64], query_up_ref[...])
        rows[k, :, 256:384] = frozen[:, 256:384] + adapter_scale * outer(
            inner[:, 64:128], key_up_ref[...]
        )
        rows[k, :, 384:] = frozen[:, 384:] + adapter_scale * outer(
            inner[:, 128:192], value_up_ref[...]
        )

    def place(count, axis):
        at = lax.broadcasted_iota(jnp.int32, (count, 64) if axis == 0 else (64, count), axis)
        return ((at >> 3) & 1) * 32 + ((at >> 4) & 3) * 8 + (at & 7)

    scale = 1.0 / math.sqrt(HEAD_DIM)
    for sequence in range(4):
        length = lengths_ref[sequence]
        across = jnp.concatenate(
            [rows[y, 16 * sequence : 16 * sequence + 16] for y in range(4)], axis=0
        )
        mine = jnp.where(first_core, rows[sequence], across)
        cosine = cosine_ref[64 * sequence : 64 * sequence + 64]
        sine = sine_ref[64 * sequence : 64 * sequence + 64]

        def rotated(value):
            return (value * cosine + pltpu.roll(value, 64, 1) * sine).astype(half)

        query = jnp.concatenate([rotated(mine[:, :128]), rotated(mine[:, 128:256])], axis=0)
        keys = rotated(mine[:, 256:384])
        values = mine[:, 384:].astype(half)
        cache_scores = outer(query, cache_ref[sequence, :, :128]) * scale
        draft_scores = outer(query, keys) * scale
        of_row = place(128, 0)
        of_column = lax.broadcasted_iota(jnp.int32, (128, 64), 1)
        of_column = ((of_column >> 3) & 1) * 32 + (of_column >> 4) * 8 + (of_column & 7)
        allowed = (of_column <= of_row) & (of_column < length)
        draft_scores = jnp.where(allowed, draft_scores, -1e30)
        highest = jnp.maximum(
            jnp.max(cache_scores, axis=1, keepdims=True),
            jnp.max(draft_scores, axis=1, keepdims=True),
        )
        cache_powers = jnp.exp(cache_scores - highest)
        draft_powers = jnp.exp(draft_scores - highest)
        bottom = jnp.sum(cache_powers, axis=1, keepdims=True) + jnp.sum(
            draft_powers, axis=1, keepdims=True
        )
        mixed = jnp.dot(
            (cache_powers / bottom).astype(half),
            cache_ref[sequence, :, 128:],
            preferred_element_type=jnp.float32,
        ) + jnp.dot(
            (draft_powers / bottom).astype(half), values, preferred_element_type=jnp.float32
        )
        row = lax.broadcasted_iota(jnp.int32, (128, 128), 0)
        row = ((row >> 3) & 1) * 32 + ((row >> 4) & 3) * 8 + (row & 7)
        mixed = (mixed * (row < length).astype(jnp.float32)).astype(half)
        found[sequence] = jnp.concatenate([mixed[:64], mixed[64:]], axis=1)

    for s in range(4):
        k = lax.rem(last + s, 4)
        at = pl.ds(pl.multiple_of(16 * k, 16), 16)
        across = jnp.concatenate([found[sequence, at] for sequence in range(4)], axis=0)
        block = jnp.where(first_core, found[k], across)
        ahead_ref[64 * s : 64 * s + 64] = block
        inner = jnp.dot(block, down_ref[...], preferred_element_type=jnp.float32).astype(half)
        for copy in range(8):
            inner_ref[8 * k + copy] = inner


def attend_rows(spot, lengths, frozen, parts, ups, cosine, sine, cache, down):
    operands = (frozen, parts, *ups, cosine, sine, cache, down)
    return pl.pallas_call(
        attend_kernel,
        in_specs=[spec_smem(), spec_smem()]
        + [pl.BlockSpec(memory_space=pltpu.VMEM)] * len(operands),
        out_specs=[pl.BlockSpec(memory_space=pltpu.VMEM)] * 2,
        out_shape=[
            jax.ShapeDtypeStruct((256, 256), jnp.bfloat16),
            jax.ShapeDtypeStruct((32, 64, 64), jnp.bfloat16),
        ],
        scratch_shapes=[
            pltpu.VMEM((4, 64, 512), jnp.float32),
            pltpu.VMEM((4, 64, 256), jnp.bfloat16),
        ],
        compiler_params=pltpu.CompilerParams(vmem_limit_bytes=24 * 2**20),
        cost_estimate=pl.CostEstimate(
            flops=2 * 512 * 320 * 256, bytes_accessed=4 * 2**20, transcendentals=512 * 320
        ),
    )(spot, lengths, *operands)


def sum_kernel(
    spot_ref,
    own_ref,
    plus_ref,
    minus_ref,
    left_ref,
    right_ref,
    parts_ref,
    up_ref,
    mine_ref,
    one_ref,
    two_ref,
    three_ref,
    total,
    inner,
):
    step = pl.program_id(0)
    at_left = step < pl.num_programs(0) // 2
    tile = own_ref.shape[1]

    @pl.when(step == 0)
    def _():
        found = parts_ref[0].astype(jnp.float32)
        for part in range(1, 32):
            found = found + parts_ref[part].astype(jnp.float32)
        inner[...] = found.astype(jnp.bfloat16)

    own = own_ref[...].astype(jnp.float32)

    @pl.when(at_left)
    def _():
        total[...] = own + minus_ref[...].astype(jnp.float32) + left_ref[...].astype(jnp.float32)

    @pl.when(jnp.logical_not(at_left))
    def _():
        total[...] = own + plus_ref[...].astype(jnp.float32) + right_ref[...].astype(jnp.float32)

    for k in range(4):
        column = spot_ref[1 + k] * 256

        @pl.when(column // tile == step)
        def _():
            at = pl.ds(pl.multiple_of(lax.rem(column, tile), 256), 256)
            total[:, at] += adapter_scale * outer(inner[...], up_ref[k])

    middle = spot_ref[0]
    for s, ref in enumerate((mine_ref, one_ref, two_ref, three_ref)):
        at = pl.ds(pl.multiple_of(16 * lax.rem(middle + s, 4), 16), 16)
        ref[...] = total[at, :].astype(ref.dtype)


def sum_rows(spot, own, plus, minus, left, right, parts, up_factor):
    tile = 1024
    steps = own.shape[1] // tile
    width = own.shape[1]
    last_left = steps // 2 - 1
    whole = pl.BlockSpec((64, tile), lambda j: (0, j))
    out = pl.BlockSpec((16, tile), lambda j: (0, j))
    return pl.pallas_call(
        sum_kernel,
        grid=(steps,),
        in_specs=[
            spec_smem(),
            whole,
            pl.BlockSpec((64, tile), lambda j: (0, jnp.maximum(j, steps // 2))),
            pl.BlockSpec((64, tile), lambda j: (0, jnp.minimum(j, last_left))),
            pl.BlockSpec((64, tile), lambda j: (0, jnp.minimum(j, last_left))),
            pl.BlockSpec((64, tile), lambda j: (0, jnp.maximum(j - steps // 2, 0))),
            pl.BlockSpec(parts.shape, lambda j: (0, 0, 0)),
            pl.BlockSpec(up_factor.shape, lambda j: (0, 0, 0)),
        ],
        out_specs=[out] * 4,
        out_shape=[jax.ShapeDtypeStruct((16, width), jnp.float32)]
        + [jax.ShapeDtypeStruct((16, width), jnp.bfloat16)] * 3,
        scratch_shapes=[
            pltpu.VMEM((64, tile), jnp.float32),
            pltpu.VMEM((64, 64), jnp.bfloat16),
        ],
        compiler_params=pltpu.CompilerParams(vmem_limit_bytes=16 * 2**20),
        cost_estimate=pl.CostEstimate(
            flops=2 * 64 * 64 * 1024, bytes_accessed=5 * 2**20, transcendentals=0
        ),
    )(spot, own, plus, minus, left, right, parts, up_factor)


def out_kernel(rows_ref, weight_ref, own_ref, plus_ref, minus_ref, left_ref, right_ref):
    at_left = pl.program_id(0) < pl.num_programs(0) // 2
    part = jnp.dot(rows_ref[...], weight_ref[...], preferred_element_type=jnp.float32)
    part = part.astype(jnp.bfloat16)
    own_ref[...] = part[:64]

    @pl.when(at_left)
    def _():
        left_ref[...] = part[64:128]
        plus_ref[...] = part[128:192]
        minus_ref[...] = part[192:]

    @pl.when(jnp.logical_not(at_left))
    def _():
        plus_ref[...] = part[64:128]
        minus_ref[...] = part[128:192]
        right_ref[...] = part[192:]


def out_pieces(rows, weight):
    tile = 2048
    depth, width = weight.shape
    steps = width // tile
    whole = pl.BlockSpec((64, tile), lambda j: (0, j))
    left = pl.BlockSpec((64, tile), lambda j: (0, jnp.minimum(j, steps // 2 - 1)))
    right = pl.BlockSpec((64, tile), lambda j: (0, jnp.maximum(j - steps // 2, 0)))
    return pl.pallas_call(
        out_kernel,
        grid=(steps,),
        in_specs=[
            pl.BlockSpec(rows.shape, lambda j: (0, 0)),
            pl.BlockSpec((depth, tile), lambda j: (0, j)),
        ],
        out_specs=[whole, whole, whole, left, right],
        out_shape=[jax.ShapeDtypeStruct((64, width), jnp.bfloat16)] * 3
        + [jax.ShapeDtypeStruct((64, width // 2), jnp.bfloat16)] * 2,
        compiler_params=pltpu.CompilerParams(vmem_limit_bytes=28 * 2**20),
        cost_estimate=pl.CostEstimate(
            flops=2 * 256 * 256 * 8192, bytes_accessed=8 * 2**20, transcendentals=0
        ),
    )(rows, weight)


def shards(
    hidden,
    norm_gain,
    start_positions,
    draft_lengths,
    query_weight,
    w_keyvalue,
    output_weight,
    kv_cache,
    a_query,
    b_query,
    a_key,
    b_key,
    a_value,
    b_value,
    a_out,
    b_out,
):
    zh, core, x, zl, y = (lax.axis_index(name) for name in AXES)
    first_core = core == 0
    last = jnp.where(first_core, x, y)
    middle = jnp.where(first_core, y, x)
    half = jnp.bfloat16

    def tp_index(k):
        return jnp.where(first_core, k * 8 + zl * 4 + y, x * 8 + zl * 4 + k)

    row_float = hidden.astype(jnp.float32)
    normed = (
        row_float
        * lax.rsqrt(jnp.mean(row_float * row_float, axis=-1, keepdims=True) + norm_eps)
        * norm_gain
    ).astype(half)

    packed = jnp.concatenate(
        [
            jnp.concatenate([a_query, a_key], axis=1),
            jnp.concatenate([a_value, a_out], axis=1),
            jnp.concatenate([b_query.T, b_out.T], axis=1),
            jnp.concatenate([b_key.T, b_value.T], axis=1),
            jnp.zeros((4, 128), half),
        ],
        axis=0,
    )
    packed, _ = lax.optimization_barrier((packed, normed))
    pooled = spread(packed, 8, pool_groups())
    wide = spread(pooled, 4, last_groups())
    pair = placed([normed, permute(normed, z_swap())], zl).reshape(16, 8192)
    met = [pair] + [permute(pair, middle_shift(s)) for s in (1, 2, 3)]
    eight = placed(met, middle).reshape(64, 8192)
    from_1 = permute(eight, last_shift(1))
    from_3 = permute(eight, last_shift(3))

    down_first = wide[:, :, 0:32].reshape(1024, 128)
    down_second = wide[:, :, 32:64].reshape(1024, 128)
    out_up = wide[:, :, 64:96, 64:].reshape(4, 256, 64)
    down_out = pooled[:, 32:64, 64:].reshape(256, 64)
    query_up = pooled[:, 64:96, :64].reshape(256, 64)
    narrow = wide[:, :, 96:100].reshape(128, 128)
    narrow = jnp.where(first_core, permute(narrow, core_swap()), narrow)
    key_up = narrow[:, :64]
    value_up = narrow[:, 64:]

    down = jnp.concatenate([down_first, down_second[:, :64]], axis=1).reshape(4, 256, 192)
    down_padded = jnp.zeros((8192, 192), half)
    for k in range(4):
        down_padded = lax.dynamic_update_slice_in_dim(down_padded, down[k], tp_index(k) * 256, 0)
    inner = dot32(eight, down_padded).astype(half)
    from_1, from_3, inner = lax.optimization_barrier((from_1, from_3, inner))
    left_2 = permute(from_1[:, :4096], last_shift(1))
    right_2 = permute(from_3[:, 4096:], last_shift(3))
    parts = spread(inner, 32, row_groups()).reshape(4, 8, 64, 192)
    frozen = project_rows(
        eight, from_1, left_2, right_2, from_3, query_weight, w_keyvalue.reshape(8192, 256)
    )
    draft_places = (
        jnp.arange(VERIFY, dtype=jnp.int32).reshape(2, 4, 8).transpose(1, 0, 2).reshape(VERIFY)
    )
    places = (start_positions[:, None] + draft_places[None, :]).reshape(-1)
    cosine, sine = turns(places, HEAD_DIM)
    spot = jnp.stack([core, last]).astype(jnp.int32)
    ahead, out_inner = attend_rows(
        spot,
        draft_lengths,
        frozen,
        parts,
        (query_up, key_up, value_up),
        cosine,
        sine,
        kv_cache.reshape(4, 256, 256),
        down_out,
    )

    own, plus, minus, left_1, right_3 = out_pieces(ahead, output_weight)
    got_plus = permute(plus, last_shift(1))
    got_minus = permute(minus, last_shift(3))
    out_inner, _ = lax.optimization_barrier((out_inner, plus))
    out_parts = lax.all_to_all(out_inner, AXES, 0, 0, axis_index_groups=row_groups())
    got_plus, got_minus = lax.optimization_barrier((got_plus, got_minus))
    got_left_1 = permute(left_1 + got_plus[:, :4096], last_shift(1))
    got_right_3 = permute(right_3 + got_minus[:, 4096:], last_shift(3))

    spot = jnp.stack([middle] + [tp_index(k) for k in range(4)]).astype(jnp.int32)
    total, *sent = sum_rows(
        spot, own, got_plus, got_minus, got_left_1, got_right_3, out_parts, out_up
    )
    for s, block in zip((1, 2, 3), sent):
        total = total + permute(block, middle_shift(s)).astype(jnp.float32)
    total = total.reshape(2, 8, 8192)
    branch = pick(total, zl) + permute(pick(total, 1 - zl).astype(half), z_swap()).astype(
        jnp.float32
    )
    return (row_float + branch).astype(half)


def solution(mesh):
    fine = Mesh(mesh.devices.reshape(4, 2, 4, 2, 4), AXES)
    both = ("x", "zl", "y", "zh", "core")
    in_specs = (
        P(AXES, None),
        P(),
        P(POOL),
        P(POOL),
        P(None, TP),
        P(TP, None, None),
        P(TP, None),
        P(POOL, None, TP, None),
        P(both, None),
        P(None, both),
        P(both, None),
        P(None, both),
        P(both, None),
        P(None, both),
        P(both, None),
        P(None, both),
    )
    out_specs = P(AXES, None)
    return jax.shard_map(shards, mesh=fine, in_specs=in_specs, out_specs=out_specs, check_vma=False)
```

```python
import math

import jax
import jax.numpy as jnp
from jax import lax
from jax.experimental import pallas as pl
from jax.experimental.pallas import tpu as pltpu
from jax.sharding import Mesh, PartitionSpec as P

VERIFY = 64
HEAD_DIM = 128

adapter_scale = 1.0
rope_base = 1000000.0
norm_eps = 1e-06

AXES = ("zh", "core", "x", "zl", "y")
TP = ("x", "zl", "y")
POOL = ("zh", "core")
SPOTS = [
    (zh, core, x, zl, y)
    for zh in range(4)
    for core in range(2)
    for x in range(4)
    for zl in range(2)
    for y in range(4)
]


def turns(places, width):
    half_dim = width // 2
    freqs = jnp.exp(
        jnp.arange(half_dim, dtype=jnp.float32) * (-2.0 * math.log(rope_base) / width)
    )
    angles = places.astype(jnp.float32)[:, None] * freqs[None, :]
    cosine, sine = jnp.cos(angles), jnp.sin(angles)
    return jnp.concatenate([cosine, cosine], axis=1), jnp.concatenate([-sine, sine], axis=1)


def dot32(left, right):
    return jnp.dot(left, right, preferred_element_type=jnp.float32)


def permute(block, source_to_target):
    return lax.ppermute(block, AXES, source_to_target)


def pairs(move):
    place = {spot: number for number, spot in enumerate(SPOTS)}
    return [(place[spot], place[move(*spot)]) for spot in SPOTS]


def last_shift(s):
    return pairs(
        lambda h, c, x, z, y: (h, c, (x + s) % 4, z, y) if c == 0 else (h, c, x, z, (y + s) % 4)
    )


def middle_shift(s):
    return pairs(
        lambda h, c, x, z, y: (h, c, x, z, (y + s) % 4) if c == 0 else (h, c, (x + s) % 4, z, y)
    )


def pool_flip(s):
    return pairs(lambda h, c, x, z, y: (h ^ s, c, x, z, y))


def y_flip(s):
    return pairs(lambda h, c, x, z, y: (h, c, x, z, y ^ s))


def z_swap():
    return pairs(lambda h, c, x, z, y: (h, c, x, 1 - z, y))


def core_swap():
    return pairs(lambda h, c, x, z, y: (h, 1 - c, x, z, y))


def placed(blocks, here):
    count = len(blocks)
    out = jnp.zeros((count,) + blocks[0].shape, blocks[0].dtype)
    for s, block in enumerate(blocks):
        out = lax.dynamic_update_index_in_dim(out, block, (here - s) % count, 0)
    return out


def gather4(block, shift, here):
    return placed([block] + [permute(block, shift(s)) for s in (1, 2, 3)], here)


def both_of(block, bit, exchange):
    other = permute(block, exchange)
    return jnp.stack([jnp.where(bit == 0, block, other), jnp.where(bit == 0, other, block)])


def pick(blocks, index):
    return lax.dynamic_index_in_dim(blocks, index, 0, keepdims=False)


def groups_of(key, order):
    found = {}
    for number, spot in enumerate(SPOTS):
        found.setdefault(key(*spot), []).append((order(*spot), number))
    return [[number for _, number in sorted(group)] for group in found.values()]


def spec_smem():
    return pl.BlockSpec(memory_space=pltpu.SMEM)


def project_kernel(
    eight_ref, one_ref, left_ref, right_ref, three_ref, query_ref, pair_ref, out_ref, total
):
    step = pl.program_id(0)
    steps = pl.num_programs(0)

    @pl.when(step == 0)
    def _():
        total[...] = jnp.zeros_like(total)

    def add(two_ref):
        rows = jnp.concatenate(
            [eight_ref[...], one_ref[...], two_ref[...], three_ref[...]], axis=0
        )
        width = query_ref.shape[1]
        total[:, :width] += jnp.dot(rows, query_ref[...], preferred_element_type=jnp.float32)
        total[:, width:] += jnp.dot(rows, pair_ref[...], preferred_element_type=jnp.float32)

    @pl.when(step < steps // 2)
    def _():
        add(left_ref)

    @pl.when(step >= steps // 2)
    def _():
        add(right_ref)

    @pl.when(step == steps - 1)
    def _():
        out_ref[...] = total[...]


def project_rows(eight, one, left_2, right_2, three, query_weight, pair_weight):
    tile = 1024
    steps = eight.shape[1] // tile
    width = query_weight.shape[1]
    whole = pl.BlockSpec((64, tile), lambda j: (0, j))
    return pl.pallas_call(
        project_kernel,
        grid=(steps,),
        in_specs=[
            whole,
            whole,
            pl.BlockSpec((64, tile), lambda j: (0, jnp.minimum(j, steps // 2 - 1))),
            pl.BlockSpec((64, tile), lambda j: (0, jnp.maximum(j - steps // 2, 0))),
            whole,
            pl.BlockSpec((tile, width), lambda j: (j, 0)),
            pl.BlockSpec((tile, width), lambda j: (j, 0)),
        ],
        out_specs=pl.BlockSpec((256, 2 * width), lambda j: (0, 0)),
        out_shape=jax.ShapeDtypeStruct((256, 2 * width), jnp.float32),
        scratch_shapes=[pltpu.VMEM((256, 2 * width), jnp.float32)],
        compiler_params=pltpu.CompilerParams(vmem_limit_bytes=12 * 2**20),
        cost_estimate=pl.CostEstimate(
            flops=2 * 256 * 512 * 8192, bytes_accessed=12 * 2**20, transcendentals=0
        ),
    )(eight, one, left_2, right_2, three, query_weight, pair_weight)


def outer(left, right):
    return lax.dot_general(
        left, right, (((1,), (1,)), ((), ())), preferred_element_type=jnp.float32
    )


def inner_kernel(spot_ref, eight_ref, one_ref, left_ref, right_ref, three_ref, *refs):
    sides = (refs[:5], refs[5:10])
    inner_ref, up_ref, total = refs[10:]
    first_core = spot_ref[0] == 0
    total[...] = jnp.zeros_like(total)

    def shard(side, s, at, zl):
        near, plus, minus, far_low, far_high = sides[side]
        if s != 2:
            return (near, plus, None, minus)[s][at, zl]
        low = far_low[lax.rem(at, 2), zl]
        high = far_high[lax.rem(at, 2), zl]
        return jnp.where(at < 2, low, high)

    for s in range(4):
        here = lax.rem(spot_ref[1] - s + 4, 4)
        for t in range(4):
            there = lax.rem(spot_ref[2] - t + 4, 4)
            x = jnp.where(first_core, here, there)
            y = jnp.where(first_core, there, here)
            for zl in range(2):
                mine = shard(0, s, there, zl)
                theirs = shard(1, t, here, zl)
                both = jnp.stack(
                    [jnp.where(first_core, mine, theirs), jnp.where(first_core, theirs, mine)],
                    axis=1,
                )
                down = both[:, :, :32].reshape(256, 128)
                rest = both[:, :, 32:].reshape(256, 128)
                index = x * 8 + zl * 4 + y
                at = pl.ds(pl.multiple_of(index * 256, 256), 256)
                halved = pl.ds(pl.multiple_of(lax.rem(index, 16) * 256, 256), 256)
                two = jnp.where(index < 16, left_ref[:, halved], right_ref[:, halved])
                rows = jnp.concatenate(
                    [eight_ref[:, at], one_ref[:, at], two, three_ref[:, at]], axis=0
                )
                total[:, :128] += jnp.dot(rows, down, preferred_element_type=jnp.float32)
                total[:, 128:] += jnp.dot(rows, rest, preferred_element_type=jnp.float32)
                up_ref[at, :] = rest
    inner_ref[...] = total[...]


def inner_rows(spot, blocks, bands):
    return pl.pallas_call(
        inner_kernel,
        in_specs=[spec_smem()]
        + [pl.BlockSpec(memory_space=pltpu.VMEM)] * (len(blocks) + len(bands)),
        out_specs=[pl.BlockSpec(memory_space=pltpu.VMEM)] * 2,
        out_shape=[
            jax.ShapeDtypeStruct((256, 256), jnp.float32),
            jax.ShapeDtypeStruct((8192, 128), jnp.bfloat16),
        ],
        scratch_shapes=[pltpu.VMEM((256, 256), jnp.float32)],
        compiler_params=pltpu.CompilerParams(vmem_limit_bytes=24 * 2**20),
        cost_estimate=pl.CostEstimate(
            flops=2 * 256 * 256 * 8192, bytes_accessed=10 * 2**20, transcendentals=0
        ),
    )(spot, *blocks, *bands)


def attend_kernel(
    spot_ref,
    lengths_ref,
    frozen_ref,
    parts_ref,
    query_up_ref,
    key_up_ref,
    value_up_ref,
    cosine_ref,
    sine_ref,
    cache_ref,
    down_ref,
    ahead_ref,
    inner_ref,
    rows,
    found,
):
    half = jnp.bfloat16
    first_core = spot_ref[0] == 0
    last = spot_ref[1]
    for s in range(4):
        k = lax.rem(last - s + 4, 4)
        inner = parts_ref[64 * s : 64 * s + 64].astype(half)
        frozen = frozen_ref[64 * s : 64 * s + 64]
        rows[k, :, :256] = frozen[:, :256] + adapter_scale * outer(inner[:, :64], query_up_ref[...])
        rows[k, :, 256:384] = frozen[:, 256:384] + adapter_scale * outer(
            inner[:, 64:128], key_up_ref[...]
        )
        rows[k, :, 384:] = frozen[:, 384:] + adapter_scale * outer(
            inner[:, 128:192], value_up_ref[...]
        )

    def place(count, axis):
        at = lax.broadcasted_iota(jnp.int32, (count, 64) if axis == 0 else (64, count), axis)
        return ((at >> 3) & 1) * 32 + ((at >> 4) & 3) * 8 + (at & 7)

    scale = 1.0 / math.sqrt(HEAD_DIM)
    for sequence in range(4):
        length = lengths_ref[sequence]
        across = jnp.concatenate(
            [rows[y, 16 * sequence : 16 * sequence + 16] for y in range(4)], axis=0
        )
        mine = jnp.where(first_core, rows[sequence], across)
        cosine = cosine_ref[64 * sequence : 64 * sequence + 64]
        sine = sine_ref[64 * sequence : 64 * sequence + 64]

        def rotated(value):
            return (value * cosine + pltpu.roll(value, 64, 1) * sine).astype(half)

        query = jnp.concatenate([rotated(mine[:, :128]), rotated(mine[:, 128:256])], axis=0)
        keys = rotated(mine[:, 256:384])
        values = mine[:, 384:].astype(half)
        cache_scores = outer(query, cache_ref[sequence, :, :128]) * scale
        draft_scores = outer(query, keys) * scale
        of_row = place(128, 0)
        of_column = lax.broadcasted_iota(jnp.int32, (128, 64), 1)
        of_column = ((of_column >> 3) & 1) * 32 + (of_column >> 4) * 8 + (of_column & 7)
        allowed = (of_column <= of_row) & (of_column < length)
        draft_scores = jnp.where(allowed, draft_scores, -1e30)
        highest = jnp.maximum(
            jnp.max(cache_scores, axis=1, keepdims=True),
            jnp.max(draft_scores, axis=1, keepdims=True),
        )
        cache_powers = jnp.exp(cache_scores - highest)
        draft_powers = jnp.exp(draft_scores - highest)
        bottom = jnp.sum(cache_powers, axis=1, keepdims=True) + jnp.sum(
            draft_powers, axis=1, keepdims=True
        )
        mixed = jnp.dot(
            (cache_powers / bottom).astype(half),
            cache_ref[sequence, :, 128:],
            preferred_element_type=jnp.float32,
        ) + jnp.dot(
            (draft_powers / bottom).astype(half), values, preferred_element_type=jnp.float32
        )
        row = lax.broadcasted_iota(jnp.int32, (128, 128), 0)
        row = ((row >> 3) & 1) * 32 + ((row >> 4) & 3) * 8 + (row & 7)
        mixed = (mixed * (row < length).astype(jnp.float32)).astype(half)
        found[sequence] = jnp.concatenate([mixed[:64], mixed[64:]], axis=1)

    for s in range(4):
        k = lax.rem(last + s, 4)
        at = pl.ds(pl.multiple_of(16 * k, 16), 16)
        across = jnp.concatenate([found[sequence, at] for sequence in range(4)], axis=0)
        block = jnp.where(first_core, found[k], across)
        ahead_ref[64 * s : 64 * s + 64] = block
        inner = jnp.dot(block, down_ref[...], preferred_element_type=jnp.float32).astype(half)
        inner_ref[64 * s : 64 * s + 64] = inner


def attend_rows(spot, lengths, frozen, parts, ups, cosine, sine, cache, down):
    operands = (frozen, parts, *ups, cosine, sine, cache, down)
    return pl.pallas_call(
        attend_kernel,
        in_specs=[spec_smem(), spec_smem()]
        + [pl.BlockSpec(memory_space=pltpu.VMEM)] * len(operands),
        out_specs=[pl.BlockSpec(memory_space=pltpu.VMEM)] * 2,
        out_shape=[
            jax.ShapeDtypeStruct((256, 256), jnp.bfloat16),
            jax.ShapeDtypeStruct((256, 128), jnp.bfloat16),
        ],
        scratch_shapes=[
            pltpu.VMEM((4, 64, 512), jnp.float32),
            pltpu.VMEM((4, 64, 256), jnp.bfloat16),
        ],
        compiler_params=pltpu.CompilerParams(vmem_limit_bytes=14 * 2**20),
        cost_estimate=pl.CostEstimate(
            flops=2 * 512 * 320 * 256, bytes_accessed=4 * 2**20, transcendentals=512 * 320
        ),
    )(spot, lengths, *operands)


def sum_kernel(
    spot_ref,
    own_ref,
    plus_ref,
    minus_ref,
    left_ref,
    right_ref,
    mine_ref,
    one_ref,
    two_ref,
    three_ref,
    total,
):
    step = pl.program_id(0)
    at_left = step < pl.num_programs(0) // 2
    own = own_ref[...].astype(jnp.float32)

    @pl.when(at_left)
    def _():
        total[...] = own + minus_ref[...].astype(jnp.float32) + left_ref[...].astype(jnp.float32)

    @pl.when(jnp.logical_not(at_left))
    def _():
        total[...] = own + plus_ref[...].astype(jnp.float32) + right_ref[...].astype(jnp.float32)

    middle = spot_ref[0]
    for s, ref in enumerate((mine_ref, one_ref, two_ref, three_ref)):
        at = pl.ds(pl.multiple_of(16 * lax.rem(middle + s, 4), 16), 16)
        ref[...] = total[at, :].astype(ref.dtype)


def sum_rows(spot, own, plus, minus, left, right):
    tile = 2048
    steps = own.shape[1] // tile
    width = own.shape[1]
    last_left = steps // 2 - 1
    whole = pl.BlockSpec((64, tile), lambda j: (0, j))
    out = pl.BlockSpec((16, tile), lambda j: (0, j))
    return pl.pallas_call(
        sum_kernel,
        grid=(steps,),
        in_specs=[
            spec_smem(),
            whole,
            pl.BlockSpec((64, tile), lambda j: (0, jnp.maximum(j, steps // 2))),
            pl.BlockSpec((64, tile), lambda j: (0, jnp.minimum(j, last_left))),
            pl.BlockSpec((64, tile), lambda j: (0, jnp.minimum(j, last_left))),
            pl.BlockSpec((64, tile), lambda j: (0, jnp.maximum(j - steps // 2, 0))),
        ],
        out_specs=[out] * 4,
        out_shape=[jax.ShapeDtypeStruct((16, width), jnp.float32)]
        + [jax.ShapeDtypeStruct((16, width), jnp.bfloat16)] * 3,
        scratch_shapes=[pltpu.VMEM((64, tile), jnp.float32)],
        compiler_params=pltpu.CompilerParams(vmem_limit_bytes=12 * 2**20),
        cost_estimate=pl.CostEstimate(
            flops=2 * 64 * 64 * 1024, bytes_accessed=5 * 2**20, transcendentals=0
        ),
    )(spot, own, plus, minus, left, right)


def out_kernel(
    rows_ref, inner_ref, weight_ref, up_ref, own_ref, plus_ref, minus_ref, left_ref, right_ref
):
    at_left = pl.program_id(0) < pl.num_programs(0) // 2
    part = jnp.dot(rows_ref[...], weight_ref[...], preferred_element_type=jnp.float32)
    part = part + adapter_scale * outer(inner_ref[:, :64], up_ref[:, 64:])
    part = part.astype(jnp.bfloat16)
    own_ref[...] = part[:64]

    @pl.when(at_left)
    def _():
        left_ref[...] = part[64:128]
        plus_ref[...] = part[128:192]
        minus_ref[...] = part[192:]

    @pl.when(jnp.logical_not(at_left))
    def _():
        plus_ref[...] = part[64:128]
        minus_ref[...] = part[128:192]
        right_ref[...] = part[192:]


def out_pieces(rows, inner, weight, up_factor):
    tile = 2048
    depth, width = weight.shape
    steps = width // tile
    whole = pl.BlockSpec((64, tile), lambda j: (0, j))
    left = pl.BlockSpec((64, tile), lambda j: (0, jnp.minimum(j, steps // 2 - 1)))
    right = pl.BlockSpec((64, tile), lambda j: (0, jnp.maximum(j - steps // 2, 0)))
    return pl.pallas_call(
        out_kernel,
        grid=(steps,),
        in_specs=[
            pl.BlockSpec(rows.shape, lambda j: (0, 0)),
            pl.BlockSpec(inner.shape, lambda j: (0, 0)),
            pl.BlockSpec((depth, tile), lambda j: (0, j)),
            pl.BlockSpec((tile, 128), lambda j: (j, 0)),
        ],
        out_specs=[whole, whole, whole, left, right],
        out_shape=[jax.ShapeDtypeStruct((64, width), jnp.bfloat16)] * 3
        + [jax.ShapeDtypeStruct((64, width // 2), jnp.bfloat16)] * 2,
        compiler_params=pltpu.CompilerParams(vmem_limit_bytes=14 * 2**20),
        cost_estimate=pl.CostEstimate(
            flops=2 * 256 * 256 * 8192, bytes_accessed=8 * 2**20, transcendentals=0
        ),
    )(rows, inner, weight, up_factor)


def shards(
    hidden,
    norm_gain,
    start_positions,
    draft_lengths,
    query_weight,
    w_keyvalue,
    output_weight,
    kv_cache,
    a_query,
    b_query,
    a_key,
    b_key,
    a_value,
    b_value,
    a_out,
    b_out,
):
    zh, core, x, zl, y = (lax.axis_index(name) for name in AXES)
    first_core = core == 0
    last = jnp.where(first_core, x, y)
    middle = jnp.where(first_core, y, x)
    half = jnp.bfloat16

    row_float = hidden.astype(jnp.float32)
    normed = (
        row_float
        * lax.rsqrt(jnp.mean(row_float * row_float, axis=-1, keepdims=True) + norm_eps)
        * norm_gain
    ).astype(half)

    packed = jnp.concatenate(
        [
            jnp.concatenate([a_query, a_key], axis=1),
            jnp.concatenate([a_value, b_out.T], axis=1),
            jnp.concatenate([a_out, b_query.T], axis=1),
            jnp.concatenate([b_key.T, b_value.T], axis=1),
            jnp.zeros((12, 128), half),
        ],
        axis=0,
    )
    packed, _ = lax.optimization_barrier((packed, normed))
    packed = both_of(packed, zh & 1, pool_flip(1))
    pair = placed([normed, permute(normed, z_swap())], zl).reshape(16, 8192)
    packed, _ = lax.optimization_barrier((packed, pair))
    met = [pair] + [permute(pair, middle_shift(s)) for s in (1, 2, 3)]
    eight = placed(met, middle).reshape(64, 8192)
    from_1 = permute(eight, last_shift(1))
    from_3 = permute(eight, last_shift(3))
    packed = both_of(packed, zh >> 1, pool_flip(2)).reshape(4, 112, 128)
    packed, _ = lax.optimization_barrier((packed, eight))
    band = packed[:, :64]
    band = placed([band, permute(band, z_swap())], zl)
    band = gather4(band, middle_shift, middle)
    from_1, from_3, band = lax.optimization_barrier((from_1, from_3, band))
    left_2 = permute(from_1[:, :4096], last_shift(1))
    right_2 = permute(from_3[:, 4096:], last_shift(3))
    band_1 = permute(band, last_shift(1))
    band_3 = permute(band, last_shift(3))

    own = jnp.swapaxes(both_of(packed[:, 64:], core, core_swap()), 0, 1).reshape(8, 48, 128)
    down_out = own[:, :32].reshape(256, 128)
    query_up = down_out[:, 64:]
    narrow = both_of(own[:, 32:36].reshape(32, 128), y & 1, y_flip(1))
    narrow = both_of(narrow, y >> 1, y_flip(2)).reshape(128, 128)
    key_up = narrow[:, :64]
    value_up = narrow[:, 64:]

    band_1, band_3 = lax.optimization_barrier((band_1, band_3))
    far_low = permute(band_1[:2], last_shift(1))
    far_high = permute(band_3[2:], last_shift(3))
    frozen = project_rows(
        eight, from_1, left_2, right_2, from_3, query_weight, w_keyvalue.reshape(8192, 256)
    )
    far_low, far_high, frozen = lax.optimization_barrier((far_low, far_high, frozen))
    bands = (band, band_1, band_3, far_low, far_high)
    bands = bands + tuple(permute(block, core_swap()) for block in bands)
    spot = jnp.stack([core, last, middle]).astype(jnp.int32)
    parts, out_up = inner_rows(spot, (eight, from_1, left_2, right_2, from_3), bands)
    draft_places = (
        jnp.arange(VERIFY, dtype=jnp.int32).reshape(2, 4, 8).transpose(1, 0, 2).reshape(VERIFY)
    )
    places = (start_positions[:, None] + draft_places[None, :]).reshape(-1)
    cosine, sine = turns(places, HEAD_DIM)
    ahead, out_inner = attend_rows(
        spot,
        draft_lengths,
        frozen,
        parts,
        (query_up, key_up, value_up),
        cosine,
        sine,
        kv_cache.reshape(4, 256, 256),
        down_out,
    )

    own, plus, minus, left_1, right_3 = out_pieces(ahead, out_inner, output_weight, out_up)
    got_plus = permute(plus, last_shift(1))
    got_minus = permute(minus, last_shift(3))
    got_plus, got_minus = lax.optimization_barrier((got_plus, got_minus))
    got_left_1 = permute(left_1 + got_plus[:, :4096], last_shift(1))
    got_right_3 = permute(right_3 + got_minus[:, 4096:], last_shift(3))

    total, *sent = sum_rows(
        middle.reshape(1), own, got_plus, got_minus, got_left_1, got_right_3
    )
    for s, block in zip((1, 2, 3), sent):
        total = total + permute(block, middle_shift(s)).astype(jnp.float32)
    total = total.reshape(2, 8, 8192)
    branch = pick(total, zl) + permute(pick(total, 1 - zl).astype(half), z_swap()).astype(
        jnp.float32
    )
    return (row_float + branch).astype(half)


def solution(mesh):
    fine = Mesh(mesh.devices.reshape(4, 2, 4, 2, 4), AXES)
    both = ("x", "zl", "y", "zh", "core")
    in_specs = (
        P(AXES, None),
        P(),
        P(POOL),
        P(POOL),
        P(None, TP),
        P(TP, None, None),
        P(TP, None),
        P(POOL, None, TP, None),
        P(both, None),
        P(None, both),
        P(both, None),
        P(None, both),
        P(both, None),
        P(None, both),
        P(both, None),
        P(None, both),
    )
    out_specs = P(AXES, None)
    return jax.shard_map(shards, mesh=fine, in_specs=in_specs, out_specs=out_specs, check_vma=False)
```

```python
import math

import jax
import jax.numpy as jnp
from jax import lax
from jax.experimental import pallas as pl
from jax.experimental.pallas import tpu as pltpu
from jax.sharding import Mesh, PartitionSpec as P

VERIFY = 64
HEAD_DIM = 128

adapter_scale = 1.0
rope_base = 1000000.0
norm_eps = 1e-06

AXES = ("zh", "core", "x", "zl", "y")
TP = ("x", "zl", "y")
POOL = ("zh", "core")
SPOTS = [
    (zh, core, x, zl, y)
    for zh in range(4)
    for core in range(2)
    for x in range(4)
    for zl in range(2)
    for y in range(4)
]


def turns(places, width):
    half_dim = width // 2
    freqs = jnp.exp(
        jnp.arange(half_dim, dtype=jnp.float32) * (-2.0 * math.log(rope_base) / width)
    )
    angles = places.astype(jnp.float32)[:, None] * freqs[None, :]
    cosine, sine = jnp.cos(angles), jnp.sin(angles)
    return jnp.concatenate([cosine, cosine], axis=1), jnp.concatenate([-sine, sine], axis=1)


def dot32(left, right):
    return jnp.dot(left, right, preferred_element_type=jnp.float32)


def permute(block, source_to_target):
    return lax.ppermute(block, AXES, source_to_target)


def pairs(move):
    place = {spot: number for number, spot in enumerate(SPOTS)}
    return [(place[spot], place[move(*spot)]) for spot in SPOTS]


def last_shift(s):
    return pairs(
        lambda h, c, x, z, y: (h, c, (x + s) % 4, z, y) if c == 0 else (h, c, x, z, (y + s) % 4)
    )


def middle_shift(s):
    return pairs(
        lambda h, c, x, z, y: (h, c, x, z, (y + s) % 4) if c == 0 else (h, c, (x + s) % 4, z, y)
    )


def pool_flip(s):
    return pairs(lambda h, c, x, z, y: (h ^ s, c, x, z, y))


def y_flip(s):
    return pairs(lambda h, c, x, z, y: (h, c, x, z, y ^ s))


def z_swap():
    return pairs(lambda h, c, x, z, y: (h, c, x, 1 - z, y))


def core_swap():
    return pairs(lambda h, c, x, z, y: (h, 1 - c, x, z, y))


def placed(blocks, here):
    count = len(blocks)
    out = jnp.zeros((count,) + blocks[0].shape, blocks[0].dtype)
    for s, block in enumerate(blocks):
        out = lax.dynamic_update_index_in_dim(out, block, (here - s) % count, 0)
    return out


def gather4(block, shift, here):
    return placed([block] + [permute(block, shift(s)) for s in (1, 2, 3)], here)


def both_of(block, bit, exchange):
    other = permute(block, exchange)
    return jnp.stack([jnp.where(bit == 0, block, other), jnp.where(bit == 0, other, block)])


def pick(blocks, index):
    return lax.dynamic_index_in_dim(blocks, index, 0, keepdims=False)


def groups_of(key, order):
    found = {}
    for number, spot in enumerate(SPOTS):
        found.setdefault(key(*spot), []).append((order(*spot), number))
    return [[number for _, number in sorted(group)] for group in found.values()]


def spec_smem():
    return pl.BlockSpec(memory_space=pltpu.SMEM)


def outer(left, right):
    return lax.dot_general(
        left, right, (((1,), (1,)), ((), ())), preferred_element_type=jnp.float32
    )


def inner_kernel(spot_ref, eight_ref, one_ref, left_ref, right_ref, three_ref, *refs):
    sides = (refs[:5], refs[5:10])
    inner_ref, up_ref, total = refs[10:]
    first_core = spot_ref[0] == 0
    total[...] = jnp.zeros_like(total)

    def shard(side, s, at, zl):
        near, plus, minus, far_low, far_high = sides[side]
        if s != 2:
            return (near, plus, None, minus)[s][at, zl]
        low = far_low[lax.rem(at, 2), zl]
        high = far_high[lax.rem(at, 2), zl]
        return jnp.where(at < 2, low, high)

    for s in range(4):
        here = lax.rem(spot_ref[1] - s + 4, 4)
        for t in range(4):
            there = lax.rem(spot_ref[2] - t + 4, 4)
            x = jnp.where(first_core, here, there)
            y = jnp.where(first_core, there, here)
            for zl in range(2):
                mine = shard(0, s, there, zl)
                theirs = shard(1, t, here, zl)
                both = jnp.stack(
                    [jnp.where(first_core, mine, theirs), jnp.where(first_core, theirs, mine)],
                    axis=1,
                )
                down = both[:, :, :32].reshape(256, 128)
                rest = both[:, :, 32:].reshape(256, 128)
                index = x * 8 + zl * 4 + y
                at = pl.ds(pl.multiple_of(index * 256, 256), 256)
                halved = pl.ds(pl.multiple_of(lax.rem(index, 16) * 256, 256), 256)
                two = jnp.where(index < 16, left_ref[:, halved], right_ref[:, halved])
                rows = jnp.concatenate(
                    [eight_ref[:, at], one_ref[:, at], two, three_ref[:, at]], axis=0
                )
                total[:, :128] += jnp.dot(rows, down, preferred_element_type=jnp.float32)
                total[:, 128:] += jnp.dot(rows, rest, preferred_element_type=jnp.float32)
                up_ref[at, :] = rest
    inner_ref[...] = total[...]


def inner_rows(spot, blocks, bands):
    return pl.pallas_call(
        inner_kernel,
        in_specs=[spec_smem()]
        + [pl.BlockSpec(memory_space=pltpu.VMEM)] * (len(blocks) + len(bands)),
        out_specs=[pl.BlockSpec(memory_space=pltpu.VMEM)] * 2,
        out_shape=[
            jax.ShapeDtypeStruct((256, 256), jnp.float32),
            jax.ShapeDtypeStruct((8192, 128), jnp.bfloat16),
        ],
        scratch_shapes=[pltpu.VMEM((256, 256), jnp.float32)],
        compiler_params=pltpu.CompilerParams(vmem_limit_bytes=24 * 2**20),
        cost_estimate=pl.CostEstimate(
            flops=2 * 256 * 256 * 8192, bytes_accessed=10 * 2**20, transcendentals=0
        ),
    )(spot, *blocks, *bands)


def attend_kernel(
    spot_ref,
    lengths_ref,
    *refs,
):
    query_refs, pair_refs = refs[:4], refs[4:8]
    parts_ref, query_up_ref, key_up_ref, value_up_ref = refs[8:12]
    cosine_ref, sine_ref, cache_ref, down_ref, ahead_ref, inner_ref, rows, found = refs[12:]
    half = jnp.bfloat16
    first_core = spot_ref[0] == 0
    last = spot_ref[1]
    for s in range(4):
        k = lax.rem(last - s + 4, 4)
        inner = parts_ref[64 * s : 64 * s + 64].astype(half)
        pair = pair_refs[s]
        rows[k, :, :256] = query_refs[s][...] + adapter_scale * outer(
            inner[:, :64], query_up_ref[...]
        )
        rows[k, :, 256:384] = pair[:, :128] + adapter_scale * outer(
            inner[:, 64:128], key_up_ref[...]
        )
        rows[k, :, 384:] = pair[:, 128:] + adapter_scale * outer(
            inner[:, 128:192], value_up_ref[...]
        )

    def place(count, axis):
        at = lax.broadcasted_iota(jnp.int32, (count, 64) if axis == 0 else (64, count), axis)
        return ((at >> 3) & 1) * 32 + ((at >> 4) & 3) * 8 + (at & 7)

    scale = 1.0 / math.sqrt(HEAD_DIM)
    for sequence in range(4):
        length = lengths_ref[sequence]
        across = jnp.concatenate(
            [rows[y, 16 * sequence : 16 * sequence + 16] for y in range(4)], axis=0
        )
        mine = jnp.where(first_core, rows[sequence], across)
        cosine = cosine_ref[64 * sequence : 64 * sequence + 64]
        sine = sine_ref[64 * sequence : 64 * sequence + 64]

        def rotated(value):
            return (value * cosine + pltpu.roll(value, 64, 1) * sine).astype(half)

        query = jnp.concatenate([rotated(mine[:, :128]), rotated(mine[:, 128:256])], axis=0)
        keys = rotated(mine[:, 256:384])
        values = mine[:, 384:].astype(half)
        cache_scores = outer(query, cache_ref[sequence, :, :128]) * scale
        draft_scores = outer(query, keys) * scale
        of_row = place(128, 0)
        of_column = lax.broadcasted_iota(jnp.int32, (128, 64), 1)
        of_column = ((of_column >> 3) & 1) * 32 + (of_column >> 4) * 8 + (of_column & 7)
        allowed = (of_column <= of_row) & (of_column < length)
        draft_scores = jnp.where(allowed, draft_scores, -1e30)
        highest = jnp.maximum(
            jnp.max(cache_scores, axis=1, keepdims=True),
            jnp.max(draft_scores, axis=1, keepdims=True),
        )
        cache_powers = jnp.exp(cache_scores - highest)
        draft_powers = jnp.exp(draft_scores - highest)
        bottom = jnp.sum(cache_powers, axis=1, keepdims=True) + jnp.sum(
            draft_powers, axis=1, keepdims=True
        )
        mixed = jnp.dot(
            (cache_powers / bottom).astype(half),
            cache_ref[sequence, :, 128:],
            preferred_element_type=jnp.float32,
        ) + jnp.dot(
            (draft_powers / bottom).astype(half), values, preferred_element_type=jnp.float32
        )
        row = lax.broadcasted_iota(jnp.int32, (128, 128), 0)
        row = ((row >> 3) & 1) * 32 + ((row >> 4) & 3) * 8 + (row & 7)
        mixed = (mixed * (row < length).astype(jnp.float32)).astype(half)
        found[sequence] = jnp.concatenate([mixed[:64], mixed[64:]], axis=1)

    for s in range(4):
        k = lax.rem(last + s, 4)
        at = pl.ds(pl.multiple_of(16 * k, 16), 16)
        across = jnp.concatenate([found[sequence, at] for sequence in range(4)], axis=0)
        block = jnp.where(first_core, found[k], across)
        ahead_ref[64 * s : 64 * s + 64] = block
        inner = jnp.dot(block, down_ref[...], preferred_element_type=jnp.float32).astype(half)
        inner_ref[64 * s : 64 * s + 64] = inner


def attend_rows(spot, lengths, frozen, parts, ups, cosine, sine, cache, down):
    operands = (*frozen, parts, *ups, cosine, sine, cache, down)
    return pl.pallas_call(
        attend_kernel,
        in_specs=[spec_smem(), spec_smem()]
        + [pl.BlockSpec(memory_space=pltpu.VMEM)] * len(operands),
        out_specs=[pl.BlockSpec(memory_space=pltpu.VMEM)] * 2,
        out_shape=[
            jax.ShapeDtypeStruct((256, 256), jnp.bfloat16),
            jax.ShapeDtypeStruct((256, 128), jnp.bfloat16),
        ],
        scratch_shapes=[
            pltpu.VMEM((4, 64, 512), jnp.float32),
            pltpu.VMEM((4, 64, 256), jnp.bfloat16),
        ],
        compiler_params=pltpu.CompilerParams(vmem_limit_bytes=14 * 2**20),
        cost_estimate=pl.CostEstimate(
            flops=2 * 512 * 320 * 256, bytes_accessed=4 * 2**20, transcendentals=512 * 320
        ),
    )(spot, lengths, *operands)


def sum_kernel(spot_ref, *refs):
    total = refs[8]
    total[...] = sum(ref[...].astype(jnp.float32) for ref in refs[:4])
    for s, ref in enumerate(refs[4:8]):
        at = pl.ds(pl.multiple_of(16 * lax.rem(spot_ref[0] + s, 4), 16), 16)
        ref[...] = total[at, :].astype(ref.dtype)


def sum_rows(spot, blocks):
    tile = 2048
    width = blocks[0].shape[1]
    return pl.pallas_call(
        sum_kernel,
        grid=(width // tile,),
        in_specs=[spec_smem()] + [pl.BlockSpec((64, tile), lambda j: (0, j))] * 4,
        out_specs=[pl.BlockSpec((16, tile), lambda j: (0, j))] * 4,
        out_shape=[jax.ShapeDtypeStruct((16, width), jnp.float32)]
        + [jax.ShapeDtypeStruct((16, width), jnp.bfloat16)] * 3,
        scratch_shapes=[pltpu.VMEM((64, tile), jnp.float32)],
        compiler_params=pltpu.CompilerParams(vmem_limit_bytes=14 * 2**20),
        cost_estimate=pl.CostEstimate(
            flops=4 * 64 * 8192, bytes_accessed=5 * 2**20, transcendentals=0
        ),
    )(spot, *blocks)


def out_kernel(rows_ref, inner_ref, weight_ref, up_ref, *out_refs):
    part = jnp.dot(rows_ref[...], weight_ref[...], preferred_element_type=jnp.float32)
    part = part + adapter_scale * outer(inner_ref[:, :64], up_ref[:, 64:])
    part = part.astype(jnp.bfloat16)
    for s in range(4):
        out_refs[s][...] = part[64 * s : 64 * s + 64]


def out_pieces(rows, inner, weight, up_factor):
    tile = 2048
    depth, width = weight.shape
    return pl.pallas_call(
        out_kernel,
        grid=(width // tile,),
        in_specs=[
            pl.BlockSpec(rows.shape, lambda j: (0, 0)),
            pl.BlockSpec(inner.shape, lambda j: (0, 0)),
            pl.BlockSpec((depth, tile), lambda j: (0, j)),
            pl.BlockSpec((tile, 128), lambda j: (j, 0)),
        ],
        out_specs=[pl.BlockSpec((64, tile), lambda j: (0, j))] * 4,
        out_shape=[jax.ShapeDtypeStruct((64, width), jnp.bfloat16)] * 4,
        compiler_params=pltpu.CompilerParams(vmem_limit_bytes=12 * 2**20),
        cost_estimate=pl.CostEstimate(
            flops=2 * 256 * 256 * 8192, bytes_accessed=8 * 2**20, transcendentals=0
        ),
    )(rows, inner, weight, up_factor)


def shards(
    hidden,
    norm_gain,
    start_positions,
    draft_lengths,
    query_weight,
    w_keyvalue,
    output_weight,
    kv_cache,
    a_query,
    b_query,
    a_key,
    b_key,
    a_value,
    b_value,
    a_out,
    b_out,
):
    zh, core, x, zl, y = (lax.axis_index(name) for name in AXES)
    first_core = core == 0
    last = jnp.where(first_core, x, y)
    middle = jnp.where(first_core, y, x)
    half = jnp.bfloat16

    row_float = hidden.astype(jnp.float32)
    normed = (
        row_float
        * lax.rsqrt(jnp.mean(row_float * row_float, axis=-1, keepdims=True) + norm_eps)
        * norm_gain
    ).astype(half)

    packed = jnp.concatenate(
        [
            jnp.concatenate([a_query, a_key], axis=1),
            jnp.concatenate([a_value, b_out.T], axis=1),
            jnp.concatenate([a_out, b_query.T], axis=1),
            jnp.concatenate([b_key.T, b_value.T], axis=1),
            jnp.zeros((12, 128), half),
        ],
        axis=0,
    )
    packed, _ = lax.optimization_barrier((packed, normed))
    packed = both_of(packed, zh & 1, pool_flip(1))
    pair = placed([normed, permute(normed, z_swap())], zl).reshape(16, 8192)
    packed, _ = lax.optimization_barrier((packed, pair))
    met = [pair] + [permute(pair, middle_shift(s)) for s in (1, 2, 3)]
    eight = placed(met, middle).reshape(64, 8192)
    from_1 = permute(eight, last_shift(1))
    from_3 = permute(eight, last_shift(3))
    packed = both_of(packed, zh >> 1, pool_flip(2)).reshape(4, 112, 128)
    packed, _ = lax.optimization_barrier((packed, eight))
    band = packed[:, :64]
    band = placed([band, permute(band, z_swap())], zl)
    band = gather4(band, middle_shift, middle)
    from_1, from_3, band = lax.optimization_barrier((from_1, from_3, band))
    late, _ = lax.optimization_barrier((packed[:, 64:], band))
    left_2 = permute(from_1[:, :4096], last_shift(1))
    right_2 = permute(from_3[:, 4096:], last_shift(3))
    band_1 = permute(band, last_shift(1))
    band_3 = permute(band, last_shift(3))

    own = jnp.swapaxes(both_of(late, core, core_swap()), 0, 1).reshape(8, 48, 128)
    down_out = own[:, :32].reshape(256, 128)
    query_up = down_out[:, 64:]
    narrow = both_of(own[:, 32:36].reshape(32, 128), y & 1, y_flip(1))
    narrow = both_of(narrow, y >> 1, y_flip(2)).reshape(128, 128)
    key_up = narrow[:, :64]
    value_up = narrow[:, 64:]

    band_1, band_3 = lax.optimization_barrier((band_1, band_3))
    far_low = permute(band_1[:2], last_shift(1))
    far_high = permute(band_3[2:], last_shift(3))
    bands, _, _ = lax.optimization_barrier(
        ((band, band_1, band_3, far_low, far_high), left_2, right_2)
    )
    frozen = []
    for weight in (query_weight, w_keyvalue[0]):
        far = dot32(left_2, weight[:4096]) + dot32(right_2, weight[4096:])
        frozen += [dot32(eight, weight), dot32(from_1, weight), far, dot32(from_3, weight)]
    bands = bands + tuple(permute(block, core_swap()) for block in bands)
    spot = jnp.stack([core, last, middle]).astype(jnp.int32)
    parts, out_up = inner_rows(spot, (eight, from_1, left_2, right_2, from_3), bands)
    draft_places = (
        jnp.arange(VERIFY, dtype=jnp.int32).reshape(2, 4, 8).transpose(1, 0, 2).reshape(VERIFY)
    )
    places = (start_positions[:, None] + draft_places[None, :]).reshape(-1)
    cosine, sine = turns(places, HEAD_DIM)
    ahead, out_inner = attend_rows(
        spot,
        draft_lengths,
        frozen,
        parts,
        (query_up, key_up, value_up),
        cosine,
        sine,
        kv_cache.reshape(4, 256, 256),
        down_out,
    )

    pieces = out_pieces(ahead, out_inner, output_weight, out_up)
    arrived = [pieces[0]] + [permute(pieces[s], last_shift(s)) for s in (2, 1, 3)]
    total, *sent = sum_rows(middle.reshape(1), arrived)
    for s, block in zip((1, 2, 3), sent):
        total = total + permute(block, middle_shift(s)).astype(jnp.float32)
    total = total.reshape(2, 8, 8192)
    branch = pick(total, zl) + permute(pick(total, 1 - zl).astype(half), z_swap()).astype(
        jnp.float32
    )
    return (row_float + branch).astype(half)


def solution(mesh):
    fine = Mesh(mesh.devices.reshape(4, 2, 4, 2, 4), AXES)
    both = ("x", "zl", "y", "zh", "core")
    in_specs = (
        P(AXES, None),
        P(),
        P(POOL),
        P(POOL),
        P(None, TP),
        P(TP, None, None),
        P(TP, None),
        P(POOL, None, TP, None),
        P(both, None),
        P(None, both),
        P(both, None),
        P(None, both),
        P(both, None),
        P(None, both),
        P(both, None),
        P(None, both),
    )
    out_specs = P(AXES, None)
    return jax.shard_map(shards, mesh=fine, in_specs=in_specs, out_specs=out_specs, check_vma=False)
```

```python
import math

import jax
import jax.numpy as jnp
from jax import lax
from jax.experimental import pallas as pl
from jax.experimental.pallas import tpu as pltpu
from jax.sharding import Mesh, PartitionSpec as P

VERIFY = 64
HEAD_DIM = 128

adapter_scale = 1.0
rope_base = 1000000.0
norm_eps = 1e-06

AXES = ("zh", "core", "x", "zl", "y")
TP = ("x", "zl", "y")
POOL = ("zh", "core")
SPOTS = [
    (zh, core, x, zl, y)
    for zh in range(4)
    for core in range(2)
    for x in range(4)
    for zl in range(2)
    for y in range(4)
]


def turns(places, width):
    half_dim = width // 2
    freqs = jnp.exp(
        jnp.arange(half_dim, dtype=jnp.float32) * (-2.0 * math.log(rope_base) / width)
    )
    angles = places.astype(jnp.float32)[:, None] * freqs[None, :]
    cosine, sine = jnp.cos(angles), jnp.sin(angles)
    return jnp.concatenate([cosine, cosine], axis=1), jnp.concatenate([-sine, sine], axis=1)


def dot32(left, right):
    return jnp.dot(left, right, preferred_element_type=jnp.float32)


def permute(block, source_to_target):
    return lax.ppermute(block, AXES, source_to_target)


def pairs(move):
    place = {spot: number for number, spot in enumerate(SPOTS)}
    return [(place[spot], place[move(*spot)]) for spot in SPOTS]


def last_shift(s):
    return pairs(
        lambda h, c, x, z, y: (h, c, (x + s) % 4, z, y) if c == 0 else (h, c, x, z, (y + s) % 4)
    )


def middle_shift(s):
    return pairs(
        lambda h, c, x, z, y: (h, c, x, z, (y + s) % 4) if c == 0 else (h, c, (x + s) % 4, z, y)
    )


def pool_flip(s):
    return pairs(lambda h, c, x, z, y: (h ^ s, c, x, z, y))


def y_flip(s):
    return pairs(lambda h, c, x, z, y: (h, c, x, z, y ^ s))


def z_swap():
    return pairs(lambda h, c, x, z, y: (h, c, x, 1 - z, y))


def core_swap():
    return pairs(lambda h, c, x, z, y: (h, 1 - c, x, z, y))


def placed(blocks, here):
    count = len(blocks)
    out = jnp.zeros((count,) + blocks[0].shape, blocks[0].dtype)
    for s, block in enumerate(blocks):
        out = lax.dynamic_update_index_in_dim(out, block, (here - s) % count, 0)
    return out


def gather4(block, shift, here):
    return placed([block] + [permute(block, shift(s)) for s in (1, 2, 3)], here)


def both_of(block, bit, exchange):
    other = permute(block, exchange)
    return jnp.stack([jnp.where(bit == 0, block, other), jnp.where(bit == 0, other, block)])


def pick(blocks, index):
    return lax.dynamic_index_in_dim(blocks, index, 0, keepdims=False)


def groups_of(key, order):
    found = {}
    for number, spot in enumerate(SPOTS):
        found.setdefault(key(*spot), []).append((order(*spot), number))
    return [[number for _, number in sorted(group)] for group in found.values()]


def spec_smem():
    return pl.BlockSpec(memory_space=pltpu.SMEM)


def outer(left, right):
    return lax.dot_general(
        left, right, (((1,), (1,)), ((), ())), preferred_element_type=jnp.float32
    )


def inner_kernel(spot_ref, eight_ref, one_ref, left_ref, right_ref, three_ref, *refs):
    sides = (refs[:5], refs[5:10])
    inner_ref, up_ref, total = refs[10:]
    first_core = spot_ref[0] == 0
    total[...] = jnp.zeros_like(total)

    def shard(side, s, at, zl):
        near, plus, minus, far_low, far_high = sides[side]
        if s != 2:
            return (near, plus, None, minus)[s][at, zl]
        low = far_low[lax.rem(at, 2), zl]
        high = far_high[lax.rem(at, 2), zl]
        return jnp.where(at < 2, low, high)

    for s in range(4):
        here = lax.rem(spot_ref[1] - s + 4, 4)
        for t in range(4):
            there = lax.rem(spot_ref[2] - t + 4, 4)
            x = jnp.where(first_core, here, there)
            y = jnp.where(first_core, there, here)
            for zl in range(2):
                mine = shard(0, s, there, zl)
                theirs = shard(1, t, here, zl)
                both = jnp.stack(
                    [jnp.where(first_core, mine, theirs), jnp.where(first_core, theirs, mine)],
                    axis=1,
                )
                down = both[:, :, :32].reshape(256, 128)
                rest = both[:, :, 32:].reshape(256, 128)
                index = x * 8 + zl * 4 + y
                at = pl.ds(pl.multiple_of(index * 256, 256), 256)
                halved = pl.ds(pl.multiple_of(lax.rem(index, 16) * 256, 256), 256)
                two = jnp.where(index < 16, left_ref[:, halved], right_ref[:, halved])
                rows = jnp.concatenate(
                    [eight_ref[:, at], one_ref[:, at], two, three_ref[:, at]], axis=0
                )
                total[:, :128] += jnp.dot(rows, down, preferred_element_type=jnp.float32)
                total[:, 128:] += jnp.dot(rows, rest, preferred_element_type=jnp.float32)
                up_ref[at, :] = rest
    inner_ref[...] = total[...]


def inner_rows(spot, blocks, bands):
    return pl.pallas_call(
        inner_kernel,
        in_specs=[spec_smem()]
        + [pl.BlockSpec(memory_space=pltpu.VMEM)] * (len(blocks) + len(bands)),
        out_specs=[pl.BlockSpec(memory_space=pltpu.VMEM)] * 2,
        out_shape=[
            jax.ShapeDtypeStruct((256, 256), jnp.float32),
            jax.ShapeDtypeStruct((8192, 128), jnp.bfloat16),
        ],
        scratch_shapes=[pltpu.VMEM((256, 256), jnp.float32)],
        compiler_params=pltpu.CompilerParams(vmem_limit_bytes=24 * 2**20),
        cost_estimate=pl.CostEstimate(
            flops=2 * 256 * 256 * 8192, bytes_accessed=10 * 2**20, transcendentals=0
        ),
    )(spot, *blocks, *bands)


def attend_kernel(
    spot_ref,
    lengths_ref,
    *refs,
):
    query_refs, pair_refs = refs[:4], refs[4:8]
    parts_ref, query_up_ref, key_up_ref, value_up_ref = refs[8:12]
    cosine_ref, sine_ref, cache_ref, down_ref, ahead_ref, inner_ref, rows, found = refs[12:]
    half = jnp.bfloat16
    first_core = spot_ref[0] == 0
    last = spot_ref[1]
    for s in range(4):
        k = lax.rem(last - s + 4, 4)
        inner = parts_ref[64 * s : 64 * s + 64].astype(half)
        pair = pair_refs[s]
        rows[k, :, :256] = query_refs[s][...] + adapter_scale * outer(
            inner[:, :64], query_up_ref[...]
        )
        rows[k, :, 256:384] = pair[:, :128] + adapter_scale * outer(
            inner[:, 64:128], key_up_ref[...]
        )
        rows[k, :, 384:] = pair[:, 128:] + adapter_scale * outer(
            inner[:, 128:192], value_up_ref[...]
        )

    def place(count, axis):
        at = lax.broadcasted_iota(jnp.int32, (count, 64) if axis == 0 else (64, count), axis)
        return ((at >> 3) & 1) * 32 + ((at >> 4) & 3) * 8 + (at & 7)

    scale = 1.0 / math.sqrt(HEAD_DIM)
    for sequence in range(4):
        length = lengths_ref[sequence]
        across = jnp.concatenate(
            [rows[y, 16 * sequence : 16 * sequence + 16] for y in range(4)], axis=0
        )
        mine = jnp.where(first_core, rows[sequence], across)
        cosine = cosine_ref[64 * sequence : 64 * sequence + 64]
        sine = sine_ref[64 * sequence : 64 * sequence + 64]

        def rotated(value):
            return (value * cosine + pltpu.roll(value, 64, 1) * sine).astype(half)

        query = jnp.concatenate([rotated(mine[:, :128]), rotated(mine[:, 128:256])], axis=0)
        keys = rotated(mine[:, 256:384])
        values = mine[:, 384:].astype(half)
        cache_scores = outer(query, cache_ref[sequence, :, :128]) * scale
        draft_scores = outer(query, keys) * scale
        of_row = place(128, 0)
        of_column = lax.broadcasted_iota(jnp.int32, (128, 64), 1)
        of_column = ((of_column >> 3) & 1) * 32 + (of_column >> 4) * 8 + (of_column & 7)
        allowed = (of_column <= of_row) & (of_column < length)
        draft_scores = jnp.where(allowed, draft_scores, -1e30)
        highest = jnp.maximum(
            jnp.max(cache_scores, axis=1, keepdims=True),
            jnp.max(draft_scores, axis=1, keepdims=True),
        )
        cache_powers = jnp.exp(cache_scores - highest)
        draft_powers = jnp.exp(draft_scores - highest)
        bottom = jnp.sum(cache_powers, axis=1, keepdims=True) + jnp.sum(
            draft_powers, axis=1, keepdims=True
        )
        mixed = jnp.dot(
            (cache_powers / bottom).astype(half),
            cache_ref[sequence, :, 128:],
            preferred_element_type=jnp.float32,
        ) + jnp.dot(
            (draft_powers / bottom).astype(half), values, preferred_element_type=jnp.float32
        )
        row = lax.broadcasted_iota(jnp.int32, (128, 128), 0)
        row = ((row >> 3) & 1) * 32 + ((row >> 4) & 3) * 8 + (row & 7)
        mixed = (mixed * (row < length).astype(jnp.float32)).astype(half)
        found[sequence] = jnp.concatenate([mixed[:64], mixed[64:]], axis=1)

    for s in range(4):
        k = lax.rem(last + s, 4)
        at = pl.ds(pl.multiple_of(16 * k, 16), 16)
        across = jnp.concatenate([found[sequence, at] for sequence in range(4)], axis=0)
        block = jnp.where(first_core, found[k], across)
        ahead_ref[64 * s : 64 * s + 64] = block
        inner = jnp.dot(block, down_ref[...], preferred_element_type=jnp.float32).astype(half)
        inner_ref[64 * s : 64 * s + 64] = inner


def attend_rows(spot, lengths, frozen, parts, ups, cosine, sine, cache, down):
    operands = (*frozen, parts, *ups, cosine, sine, cache, down)
    return pl.pallas_call(
        attend_kernel,
        in_specs=[spec_smem(), spec_smem()]
        + [pl.BlockSpec(memory_space=pltpu.VMEM)] * len(operands),
        out_specs=[pl.BlockSpec(memory_space=pltpu.VMEM)] * 2,
        out_shape=[
            jax.ShapeDtypeStruct((256, 256), jnp.bfloat16),
            jax.ShapeDtypeStruct((256, 128), jnp.bfloat16),
        ],
        scratch_shapes=[
            pltpu.VMEM((4, 64, 512), jnp.float32),
            pltpu.VMEM((4, 64, 256), jnp.bfloat16),
        ],
        compiler_params=pltpu.CompilerParams(vmem_limit_bytes=14 * 2**20),
        cost_estimate=pl.CostEstimate(
            flops=2 * 512 * 320 * 256, bytes_accessed=4 * 2**20, transcendentals=512 * 320
        ),
    )(spot, lengths, *operands)


def sum_kernel(spot_ref, *refs):
    total = refs[8]
    tile = total.shape[1]
    for j in range(refs[0].shape[1] // tile):
        along = slice(tile * j, tile * j + tile)
        total[...] = sum(ref[:, along].astype(jnp.float32) for ref in refs[:4])
        for s, ref in enumerate(refs[4:8]):
            at = pl.ds(pl.multiple_of(16 * lax.rem(spot_ref[0] + s, 4), 16), 16)
            ref[:, along] = total[at, :].astype(ref.dtype)


def sum_rows(spot, blocks):
    width = blocks[0].shape[1]
    return pl.pallas_call(
        sum_kernel,
        in_specs=[spec_smem()] + [pl.BlockSpec(memory_space=pltpu.VMEM)] * 4,
        out_specs=[pl.BlockSpec(memory_space=pltpu.VMEM)] * 4,
        out_shape=[jax.ShapeDtypeStruct((16, width), jnp.float32)]
        + [jax.ShapeDtypeStruct((16, width), jnp.bfloat16)] * 3,
        scratch_shapes=[pltpu.VMEM((64, 2048), jnp.float32)],
        compiler_params=pltpu.CompilerParams(vmem_limit_bytes=14 * 2**20),
        cost_estimate=pl.CostEstimate(
            flops=4 * 64 * 8192, bytes_accessed=5 * 2**20, transcendentals=0
        ),
    )(spot, *blocks)


def out_kernel(rows_ref, inner_ref, weight_ref, up_ref, *out_refs):
    tile = 2048
    for j in range(weight_ref.shape[1] // tile):
        at = slice(tile * j, tile * j + tile)
        part = jnp.dot(rows_ref[...], weight_ref[:, at], preferred_element_type=jnp.float32)
        part = part + adapter_scale * outer(inner_ref[:, :64], up_ref[at, 64:])
        part = part.astype(jnp.bfloat16)
        for s in range(4):
            out_refs[s][:, at] = part[64 * s : 64 * s + 64]


def out_pieces(rows, inner, weight, up_factor):
    return pl.pallas_call(
        out_kernel,
        in_specs=[pl.BlockSpec(memory_space=pltpu.VMEM)] * 4,
        out_specs=[pl.BlockSpec(memory_space=pltpu.VMEM)] * 4,
        out_shape=[jax.ShapeDtypeStruct((64, weight.shape[1]), jnp.bfloat16)] * 4,
        compiler_params=pltpu.CompilerParams(vmem_limit_bytes=20 * 2**20),
        cost_estimate=pl.CostEstimate(
            flops=2 * 256 * 256 * 8192, bytes_accessed=8 * 2**20, transcendentals=0
        ),
    )(rows, inner, weight, up_factor)


def shards(
    hidden,
    norm_gain,
    start_positions,
    draft_lengths,
    query_weight,
    w_keyvalue,
    output_weight,
    kv_cache,
    a_query,
    b_query,
    a_key,
    b_key,
    a_value,
    b_value,
    a_out,
    b_out,
):
    zh, core, x, zl, y = (lax.axis_index(name) for name in AXES)
    first_core = core == 0
    last = jnp.where(first_core, x, y)
    middle = jnp.where(first_core, y, x)
    half = jnp.bfloat16

    row_float = hidden.astype(jnp.float32)
    normed = (
        row_float
        * lax.rsqrt(jnp.mean(row_float * row_float, axis=-1, keepdims=True) + norm_eps)
        * norm_gain
    ).astype(half)

    packed = jnp.concatenate(
        [
            jnp.concatenate([a_query, a_key], axis=1),
            jnp.concatenate([a_value, b_out.T], axis=1),
            jnp.concatenate([a_out, b_query.T], axis=1),
            jnp.concatenate([b_key.T, b_value.T], axis=1),
            jnp.zeros((12, 128), half),
        ],
        axis=0,
    )
    packed, _ = lax.optimization_barrier((packed, normed))
    packed = both_of(packed, zh & 1, pool_flip(1))
    pair = placed([normed, permute(normed, z_swap())], zl).reshape(16, 8192)
    packed, _ = lax.optimization_barrier((packed, pair))
    met = [pair] + [permute(pair, middle_shift(s)) for s in (1, 2, 3)]
    eight = placed(met, middle).reshape(64, 8192)
    from_1 = permute(eight, last_shift(1))
    from_3 = permute(eight, last_shift(3))
    packed = both_of(packed, zh >> 1, pool_flip(2)).reshape(4, 112, 128)
    packed, _ = lax.optimization_barrier((packed, eight))
    band = packed[:, :64]
    band = placed([band, permute(band, z_swap())], zl)
    band = gather4(band, middle_shift, middle)
    from_1, from_3, band = lax.optimization_barrier((from_1, from_3, band))
    late, _ = lax.optimization_barrier((packed[:, 64:], band))
    left_2 = permute(from_1[:, :4096], last_shift(1))
    right_2 = permute(from_3[:, 4096:], last_shift(3))
    band_1 = permute(band, last_shift(1))
    band_3 = permute(band, last_shift(3))

    own = jnp.swapaxes(both_of(late, core, core_swap()), 0, 1).reshape(8, 48, 128)
    down_out = own[:, :32].reshape(256, 128)
    query_up = down_out[:, 64:]
    narrow = both_of(own[:, 32:36].reshape(32, 128), y & 1, y_flip(1))
    narrow = both_of(narrow, y >> 1, y_flip(2)).reshape(128, 128)
    key_up = narrow[:, :64]
    value_up = narrow[:, 64:]

    band_1, band_3 = lax.optimization_barrier((band_1, band_3))
    far_low = permute(band_1[:2], last_shift(1))
    far_high = permute(band_3[2:], last_shift(3))
    bands, _, _ = lax.optimization_barrier(
        ((band, band_1, band_3, far_low, far_high), left_2, right_2)
    )
    frozen = []
    for weight in (query_weight, w_keyvalue[0]):
        far = dot32(left_2, weight[:4096]) + dot32(right_2, weight[4096:])
        frozen += [dot32(eight, weight), dot32(from_1, weight), far, dot32(from_3, weight)]
    bands = bands + tuple(permute(block, core_swap()) for block in bands)
    spot = jnp.stack([core, last, middle]).astype(jnp.int32)
    parts, out_up = inner_rows(spot, (eight, from_1, left_2, right_2, from_3), bands)
    draft_places = (
        jnp.arange(VERIFY, dtype=jnp.int32).reshape(2, 4, 8).transpose(1, 0, 2).reshape(VERIFY)
    )
    places = (start_positions[:, None] + draft_places[None, :]).reshape(-1)
    cosine, sine = turns(places, HEAD_DIM)
    ahead, out_inner = attend_rows(
        spot,
        draft_lengths,
        frozen,
        parts,
        (query_up, key_up, value_up),
        cosine,
        sine,
        kv_cache.reshape(4, 256, 256),
        down_out,
    )

    pieces = out_pieces(ahead, out_inner, output_weight, out_up)
    arrived = [pieces[0]] + [permute(pieces[s], last_shift(s)) for s in (2, 1, 3)]
    total, *sent = sum_rows(middle.reshape(1), arrived)
    for s, block in zip((1, 2, 3), sent):
        total = total + permute(block, middle_shift(s)).astype(jnp.float32)
    total = total.reshape(2, 8, 8192)
    branch = pick(total, zl) + permute(pick(total, 1 - zl).astype(half), z_swap()).astype(
        jnp.float32
    )
    return (row_float + branch).astype(half)


def solution(mesh):
    fine = Mesh(mesh.devices.reshape(4, 2, 4, 2, 4), AXES)
    both = ("x", "zl", "y", "zh", "core")
    in_specs = (
        P(AXES, None),
        P(),
        P(POOL),
        P(POOL),
        P(None, TP),
        P(TP, None, None),
        P(TP, None),
        P(POOL, None, TP, None),
        P(both, None),
        P(None, both),
        P(both, None),
        P(None, both),
        P(both, None),
        P(None, both),
        P(both, None),
        P(None, both),
    )
    out_specs = P(AXES, None)
    return jax.shard_map(shards, mesh=fine, in_specs=in_specs, out_specs=out_specs, check_vma=False)
```

```python
import math

import jax
import jax.numpy as jnp
from jax import lax
from jax.experimental import pallas as pl
from jax.experimental.pallas import tpu as pltpu
from jax.sharding import Mesh, PartitionSpec as P

VERIFY = 64
HEAD_DIM = 128

adapter_scale = 1.0
rope_base = 1000000.0
norm_eps = 1e-06

AXES = ("zh", "core", "x", "zl", "y")
TP = ("x", "zl", "y")
POOL = ("zh", "core")
SPOTS = [
    (zh, core, x, zl, y)
    for zh in range(4)
    for core in range(2)
    for x in range(4)
    for zl in range(2)
    for y in range(4)
]


def turns(places, width):
    half_dim = width // 2
    freqs = jnp.exp(
        jnp.arange(half_dim, dtype=jnp.float32) * (-2.0 * math.log(rope_base) / width)
    )
    angles = places.astype(jnp.float32)[:, None] * freqs[None, :]
    cosine, sine = jnp.cos(angles), jnp.sin(angles)
    return jnp.concatenate([cosine, cosine], axis=1), jnp.concatenate([-sine, sine], axis=1)


def dot32(left, right):
    return jnp.dot(left, right, preferred_element_type=jnp.float32)


def permute(block, source_to_target):
    return lax.ppermute(block, AXES, source_to_target)


def pairs(move):
    place = {spot: number for number, spot in enumerate(SPOTS)}
    return [(place[spot], place[move(*spot)]) for spot in SPOTS]


def last_shift(s):
    return pairs(
        lambda h, c, x, z, y: (h, c, (x + s) % 4, z, y) if c == 0 else (h, c, x, z, (y + s) % 4)
    )


def middle_shift(s):
    return pairs(
        lambda h, c, x, z, y: (h, c, x, z, (y + s) % 4) if c == 0 else (h, c, (x + s) % 4, z, y)
    )


def pool_flip(s):
    return pairs(lambda h, c, x, z, y: (h ^ s, c, x, z, y))


def y_flip(s):
    return pairs(lambda h, c, x, z, y: (h, c, x, z, y ^ s))


def z_swap():
    return pairs(lambda h, c, x, z, y: (h, c, x, 1 - z, y))


def core_swap():
    return pairs(lambda h, c, x, z, y: (h, 1 - c, x, z, y))


def placed(blocks, here):
    count = len(blocks)
    out = jnp.zeros((count,) + blocks[0].shape, blocks[0].dtype)
    for s, block in enumerate(blocks):
        out = lax.dynamic_update_index_in_dim(out, block, (here - s) % count, 0)
    return out


def gather4(block, shift, here):
    return placed([block] + [permute(block, shift(s)) for s in (1, 2, 3)], here)


def both_of(block, bit, exchange):
    other = permute(block, exchange)
    return jnp.stack([jnp.where(bit == 0, block, other), jnp.where(bit == 0, other, block)])


def pick(blocks, index):
    return lax.dynamic_index_in_dim(blocks, index, 0, keepdims=False)


def groups_of(key, order):
    found = {}
    for number, spot in enumerate(SPOTS):
        found.setdefault(key(*spot), []).append((order(*spot), number))
    return [[number for _, number in sorted(group)] for group in found.values()]


def spec_smem():
    return pl.BlockSpec(memory_space=pltpu.SMEM)


def outer(left, right):
    return lax.dot_general(
        left, right, (((1,), (1,)), ((), ())), preferred_element_type=jnp.float32
    )


def inner_kernel(spot_ref, eight_ref, one_ref, left_ref, right_ref, three_ref, *refs):
    sides = (refs[:5], refs[5:10])
    inner_ref, up_ref, total = refs[10:]
    first_core = spot_ref[0] == 0
    total[...] = jnp.zeros_like(total)

    def shard(side, s, at, zl):
        near, plus, minus, far_low, far_high = sides[side]
        if s != 2:
            return (near, plus, None, minus)[s][at, zl]
        low = far_low[lax.rem(at, 2), zl]
        high = far_high[lax.rem(at, 2), zl]
        return jnp.where(at < 2, low, high)

    for s in range(4):
        here = lax.rem(spot_ref[1] - s + 4, 4)
        for t in range(4):
            there = lax.rem(spot_ref[2] - t + 4, 4)
            x = jnp.where(first_core, here, there)
            y = jnp.where(first_core, there, here)
            rows, factors = [], []
            for zl in range(2):
                mine = shard(0, s, there, zl)
                theirs = shard(1, t, here, zl)
                both = jnp.stack(
                    [jnp.where(first_core, mine, theirs), jnp.where(first_core, theirs, mine)],
                    axis=1,
                )
                rest = both[:, :, 32:].reshape(256, 128)
                factors.append(jnp.concatenate([both[:, :, :32].reshape(256, 128), rest], axis=1))
                index = x * 8 + zl * 4 + y
                at = pl.ds(pl.multiple_of(index * 256, 256), 256)
                halved = pl.ds(pl.multiple_of(lax.rem(index, 16) * 256, 256), 256)
                two = jnp.where(index < 16, left_ref[:, halved], right_ref[:, halved])
                rows.append(
                    jnp.concatenate([eight_ref[:, at], one_ref[:, at], two, three_ref[:, at]], axis=0)
                )
                up_ref[at, :] = rest
            total[...] += jnp.dot(
                jnp.concatenate(rows, axis=1),
                jnp.concatenate(factors, axis=0),
                preferred_element_type=jnp.float32,
            )
    inner_ref[...] = total[...]


def inner_rows(spot, blocks, bands):
    return pl.pallas_call(
        inner_kernel,
        in_specs=[spec_smem()]
        + [pl.BlockSpec(memory_space=pltpu.VMEM)] * (len(blocks) + len(bands)),
        out_specs=[pl.BlockSpec(memory_space=pltpu.VMEM)] * 2,
        out_shape=[
            jax.ShapeDtypeStruct((256, 256), jnp.float32),
            jax.ShapeDtypeStruct((8192, 128), jnp.bfloat16),
        ],
        scratch_shapes=[pltpu.VMEM((256, 256), jnp.float32)],
        compiler_params=pltpu.CompilerParams(vmem_limit_bytes=24 * 2**20),
        cost_estimate=pl.CostEstimate(
            flops=2 * 256 * 256 * 8192, bytes_accessed=10 * 2**20, transcendentals=0
        ),
    )(spot, *blocks, *bands)


def attend_kernel(
    spot_ref,
    lengths_ref,
    *refs,
):
    query_refs, pair_refs = refs[:4], refs[4:8]
    parts_ref, query_up_ref, key_up_ref, value_up_ref = refs[8:12]
    cosine_ref, sine_ref, cache_ref, down_ref, ahead_ref, inner_ref, rows, found = refs[12:]
    half = jnp.bfloat16
    first_core = spot_ref[0] == 0
    last = spot_ref[1]
    for s in range(4):
        k = lax.rem(last - s + 4, 4)
        inner = parts_ref[64 * s : 64 * s + 64].astype(half)
        pair = pair_refs[s]
        rows[k, :, :256] = query_refs[s][...] + adapter_scale * outer(
            inner[:, :64], query_up_ref[...]
        )
        rows[k, :, 256:384] = pair[:, :128] + adapter_scale * outer(
            inner[:, 64:128], key_up_ref[...]
        )
        rows[k, :, 384:] = pair[:, 128:] + adapter_scale * outer(
            inner[:, 128:192], value_up_ref[...]
        )

    def place(count, axis):
        at = lax.broadcasted_iota(jnp.int32, (count, 64) if axis == 0 else (64, count), axis)
        return ((at >> 3) & 1) * 32 + ((at >> 4) & 3) * 8 + (at & 7)

    scale = 1.0 / math.sqrt(HEAD_DIM)
    for sequence in range(4):
        length = lengths_ref[sequence]
        across = jnp.concatenate(
            [rows[y, 16 * sequence : 16 * sequence + 16] for y in range(4)], axis=0
        )
        mine = jnp.where(first_core, rows[sequence], across)
        cosine = cosine_ref[64 * sequence : 64 * sequence + 64]
        sine = sine_ref[64 * sequence : 64 * sequence + 64]

        def rotated(value):
            return (value * cosine + pltpu.roll(value, 64, 1) * sine).astype(half)

        query = jnp.concatenate([rotated(mine[:, :128]), rotated(mine[:, 128:256])], axis=0)
        keys = rotated(mine[:, 256:384])
        values = mine[:, 384:].astype(half)
        cache_scores = outer(query, cache_ref[sequence, :, :128]) * scale
        draft_scores = outer(query, keys) * scale
        of_row = place(128, 0)
        of_column = lax.broadcasted_iota(jnp.int32, (128, 64), 1)
        of_column = ((of_column >> 3) & 1) * 32 + (of_column >> 4) * 8 + (of_column & 7)
        allowed = (of_column <= of_row) & (of_column < length)
        draft_scores = jnp.where(allowed, draft_scores, -1e30)
        highest = jnp.maximum(
            jnp.max(cache_scores, axis=1, keepdims=True),
            jnp.max(draft_scores, axis=1, keepdims=True),
        )
        cache_powers = jnp.exp(cache_scores - highest)
        draft_powers = jnp.exp(draft_scores - highest)
        bottom = jnp.sum(cache_powers, axis=1, keepdims=True) + jnp.sum(
            draft_powers, axis=1, keepdims=True
        )
        mixed = jnp.dot(
            (cache_powers / bottom).astype(half),
            cache_ref[sequence, :, 128:],
            preferred_element_type=jnp.float32,
        ) + jnp.dot(
            (draft_powers / bottom).astype(half), values, preferred_element_type=jnp.float32
        )
        row = lax.broadcasted_iota(jnp.int32, (128, 128), 0)
        row = ((row >> 3) & 1) * 32 + ((row >> 4) & 3) * 8 + (row & 7)
        mixed = (mixed * (row < length).astype(jnp.float32)).astype(half)
        found[sequence] = jnp.concatenate([mixed[:64], mixed[64:]], axis=1)

    for s in range(4):
        k = lax.rem(last + s, 4)
        at = pl.ds(pl.multiple_of(16 * k, 16), 16)
        across = jnp.concatenate([found[sequence, at] for sequence in range(4)], axis=0)
        block = jnp.where(first_core, found[k], across)
        ahead_ref[64 * s : 64 * s + 64] = block
        inner = jnp.dot(block, down_ref[...], preferred_element_type=jnp.float32).astype(half)
        inner_ref[64 * s : 64 * s + 64] = inner


def attend_rows(spot, lengths, frozen, parts, ups, cosine, sine, cache, down):
    operands = (*frozen, parts, *ups, cosine, sine, cache, down)
    return pl.pallas_call(
        attend_kernel,
        in_specs=[spec_smem(), spec_smem()]
        + [pl.BlockSpec(memory_space=pltpu.VMEM)] * len(operands),
        out_specs=[pl.BlockSpec(memory_space=pltpu.VMEM)] * 2,
        out_shape=[
            jax.ShapeDtypeStruct((256, 256), jnp.bfloat16),
            jax.ShapeDtypeStruct((256, 128), jnp.bfloat16),
        ],
        scratch_shapes=[
            pltpu.VMEM((4, 64, 512), jnp.float32),
            pltpu.VMEM((4, 64, 256), jnp.bfloat16),
        ],
        compiler_params=pltpu.CompilerParams(vmem_limit_bytes=14 * 2**20),
        cost_estimate=pl.CostEstimate(
            flops=2 * 512 * 320 * 256, bytes_accessed=4 * 2**20, transcendentals=512 * 320
        ),
    )(spot, lengths, *operands)


def sum_kernel(spot_ref, *refs):
    total = refs[8]
    tile = total.shape[1]
    for j in range(refs[0].shape[1] // tile):
        along = slice(tile * j, tile * j + tile)
        total[...] = sum(ref[:, along].astype(jnp.float32) for ref in refs[:4])
        for s, ref in enumerate(refs[4:8]):
            at = pl.ds(pl.multiple_of(16 * lax.rem(spot_ref[0] + s, 4), 16), 16)
            ref[:, along] = total[at, :].astype(ref.dtype)


def sum_rows(spot, blocks):
    width = blocks[0].shape[1]
    return pl.pallas_call(
        sum_kernel,
        in_specs=[spec_smem()] + [pl.BlockSpec(memory_space=pltpu.VMEM)] * 4,
        out_specs=[pl.BlockSpec(memory_space=pltpu.VMEM)] * 4,
        out_shape=[jax.ShapeDtypeStruct((16, width), jnp.float32)]
        + [jax.ShapeDtypeStruct((16, width), jnp.bfloat16)] * 3,
        scratch_shapes=[pltpu.VMEM((64, 2048), jnp.float32)],
        compiler_params=pltpu.CompilerParams(vmem_limit_bytes=14 * 2**20),
        cost_estimate=pl.CostEstimate(
            flops=4 * 64 * 8192, bytes_accessed=5 * 2**20, transcendentals=0
        ),
    )(spot, *blocks)


def out_kernel(rows_ref, inner_ref, weight_ref, up_ref, *out_refs):
    tile = 2048
    for j in range(weight_ref.shape[1] // tile):
        at = slice(tile * j, tile * j + tile)
        part = jnp.dot(rows_ref[...], weight_ref[:, at], preferred_element_type=jnp.float32)
        part = part + adapter_scale * outer(inner_ref[:, :64], up_ref[at, 64:])
        part = part.astype(jnp.bfloat16)
        for s in range(4):
            out_refs[s][:, at] = part[64 * s : 64 * s + 64]


def out_pieces(rows, inner, weight, up_factor):
    return pl.pallas_call(
        out_kernel,
        in_specs=[pl.BlockSpec(memory_space=pltpu.VMEM)] * 4,
        out_specs=[pl.BlockSpec(memory_space=pltpu.VMEM)] * 4,
        out_shape=[jax.ShapeDtypeStruct((64, weight.shape[1]), jnp.bfloat16)] * 4,
        compiler_params=pltpu.CompilerParams(vmem_limit_bytes=20 * 2**20),
        cost_estimate=pl.CostEstimate(
            flops=2 * 256 * 256 * 8192, bytes_accessed=8 * 2**20, transcendentals=0
        ),
    )(rows, inner, weight, up_factor)


def shards(
    hidden,
    norm_gain,
    start_positions,
    draft_lengths,
    query_weight,
    w_keyvalue,
    output_weight,
    kv_cache,
    a_query,
    b_query,
    a_key,
    b_key,
    a_value,
    b_value,
    a_out,
    b_out,
):
    zh, core, x, zl, y = (lax.axis_index(name) for name in AXES)
    first_core = core == 0
    last = jnp.where(first_core, x, y)
    middle = jnp.where(first_core, y, x)
    half = jnp.bfloat16

    row_float = hidden.astype(jnp.float32)
    normed = (
        row_float
        * lax.rsqrt(jnp.mean(row_float * row_float, axis=-1, keepdims=True) + norm_eps)
        * norm_gain
    ).astype(half)

    packed = jnp.concatenate(
        [
            jnp.concatenate([a_query, a_key], axis=1),
            jnp.concatenate([a_value, b_out.T], axis=1),
            jnp.concatenate([a_out, b_query.T], axis=1),
            jnp.concatenate([b_key.T, b_value.T], axis=1),
            jnp.zeros((12, 128), half),
        ],
        axis=0,
    )
    packed, _ = lax.optimization_barrier((packed, normed))
    packed = both_of(packed, zh & 1, pool_flip(1))
    pair = placed([normed, permute(normed, z_swap())], zl).reshape(16, 8192)
    packed, _ = lax.optimization_barrier((packed, pair))
    met = [pair] + [permute(pair, middle_shift(s)) for s in (1, 2, 3)]
    eight = placed(met, middle).reshape(64, 8192)
    from_1 = permute(eight, last_shift(1))
    from_3 = permute(eight, last_shift(3))
    packed = both_of(packed, zh >> 1, pool_flip(2)).reshape(4, 112, 128)
    packed, _ = lax.optimization_barrier((packed, eight))
    band = packed[:, :64]
    band = placed([band, permute(band, z_swap())], zl)
    band = gather4(band, middle_shift, middle)
    from_1, from_3, band = lax.optimization_barrier((from_1, from_3, band))
    late, _ = lax.optimization_barrier((packed[:, 64:], band))
    left_2 = permute(from_1[:, :4096], last_shift(1))
    right_2 = permute(from_3[:, 4096:], last_shift(3))
    band_1 = permute(band, last_shift(1))
    band_3 = permute(band, last_shift(3))

    own = jnp.swapaxes(both_of(late, core, core_swap()), 0, 1).reshape(8, 48, 128)
    down_out = own[:, :32].reshape(256, 128)
    query_up = down_out[:, 64:]
    narrow = both_of(own[:, 32:36].reshape(32, 128), y & 1, y_flip(1))
    narrow = both_of(narrow, y >> 1, y_flip(2)).reshape(128, 128)
    key_up = narrow[:, :64]
    value_up = narrow[:, 64:]

    band_1, band_3 = lax.optimization_barrier((band_1, band_3))
    far_low = permute(band_1[:2], last_shift(1))
    far_high = permute(band_3[2:], last_shift(3))
    bands, _, _ = lax.optimization_barrier(
        ((band, band_1, band_3, far_low, far_high), left_2, right_2)
    )
    frozen = []
    for weight in (query_weight, w_keyvalue[0]):
        far = dot32(left_2, weight[:4096]) + dot32(right_2, weight[4096:])
        frozen += [dot32(eight, weight), dot32(from_1, weight), far, dot32(from_3, weight)]
    bands = bands + tuple(permute(block, core_swap()) for block in bands)
    spot = jnp.stack([core, last, middle]).astype(jnp.int32)
    parts, out_up = inner_rows(spot, (eight, from_1, left_2, right_2, from_3), bands)
    draft_places = (
        jnp.arange(VERIFY, dtype=jnp.int32).reshape(2, 4, 8).transpose(1, 0, 2).reshape(VERIFY)
    )
    places = (start_positions[:, None] + draft_places[None, :]).reshape(-1)
    cosine, sine = turns(places, HEAD_DIM)
    ahead, out_inner = attend_rows(
        spot,
        draft_lengths,
        frozen,
        parts,
        (query_up, key_up, value_up),
        cosine,
        sine,
        kv_cache.reshape(4, 256, 256),
        down_out,
    )

    pieces = out_pieces(ahead, out_inner, output_weight, out_up)
    arrived = [pieces[0]] + [permute(pieces[s], last_shift(s)) for s in (2, 1, 3)]
    total, *sent = sum_rows(middle.reshape(1), arrived)
    for s, block in zip((1, 2, 3), sent):
        total = total + permute(block, middle_shift(s)).astype(jnp.float32)
    total = total.reshape(2, 8, 8192)
    branch = pick(total, zl) + permute(pick(total, 1 - zl).astype(half), z_swap()).astype(
        jnp.float32
    )
    return (row_float + branch).astype(half)


def solution(mesh):
    fine = Mesh(mesh.devices.reshape(4, 2, 4, 2, 4), AXES)
    both = ("x", "zl", "y", "zh", "core")
    in_specs = (
        P(AXES, None),
        P(),
        P(POOL),
        P(POOL),
        P(None, TP),
        P(TP, None, None),
        P(TP, None),
        P(POOL, None, TP, None),
        P(both, None),
        P(None, both),
        P(both, None),
        P(None, both),
        P(both, None),
        P(None, both),
        P(both, None),
        P(None, both),
    )
    out_specs = P(AXES, None)
    return jax.shard_map(shards, mesh=fine, in_specs=in_specs, out_specs=out_specs, check_vma=False)
```
